512 devices in a mesh: pp: 16 (over z_lo, x), ep: 32 (over z_hi, y, core).
Axes of the slice: x: 4, y: 8, z: 8 (z_hi: 2, z_lo: 4; z = z_hi * 4 + z_lo), core: 2. Of those that a mesh axis runs over, the one named last changes fastest.
Arguments:
- rising_state: bfloat16 [16, 2048, 3584], P('pp', 'ep'), may hold values from -6 to 6
- falling_state: bfloat16 [16, 2048, 3584], P('pp', 'ep'), may hold values from -6 to 6
- rising_ids: int32 [3, 16, 2048, 8], P(None, 'pp', 'ep'), may hold values from 0 to 255, all different within a row; in each aligned block of 64 rows (0 to 63, 64 to 127, ..., all dimensions but the last counted through in order) at most 4 rows name the same one
- falling_ids: int32 [3, 16, 2048, 8], P(None, 'pp', 'ep'), may hold values from 0 to 255, all different within a row; in each aligned block of 64 rows (0 to 63, 64 to 127, ..., all dimensions but the last counted through in order) at most 4 rows name the same one
- norm_gain: float32 [16, 3584], P('pp'), may hold values from 0.1 to 1.9
- router: bfloat16 [16, 256, 3584], P('pp', 'ep'), may hold values from -0.09375 to 0.09375
- w_gate: bfloat16 [16, 3584, 4096], P('pp', None, 'ep'), may hold values from -0.09375 to 0.09375
- w_up: bfloat16 [16, 3584, 4096], P('pp', None, 'ep'), may hold values from -0.09375 to 0.09375
- w_down: bfloat16 [16, 4096, 3584], P('pp', 'ep'), may hold values from -0.1875 to 0.1875
Outputs:
- rising_out: bfloat16 [16, 2048, 3584], P('pp', 'ep')
- falling_out: bfloat16 [16, 2048, 3584], P('pp', 'ep')
The draws below stay inside these ranges and needn't reach their ends.
Inputs may be any that keep to these rules, and one draw needn't show every extreme that they name: `rising_ids`: each row names 8 different experts; within one step and rank, the 64 rows of one device name no expert more than 4 times. `falling_ids`: each row names 8 different experts; within one step and rank, the 64 rows of one device name no expert more than 4 times.
All inputs are finite; a program needn't handle non-finite values.
Results may differ from the reference program's by a relative error of at most 0.002.
Values may be sent and summed in bfloat16 or wider, within the bound.
A program may use at most 64 MiB of HBM per device.

```python
import math
import jax
import jax.numpy as jnp
import numpy as np
from jax import lax

D = 3584
EXPERTS = 256
EXP_WIDTH = 1024
TOP = 8
SPLIT = 8
STEPS = 3
HALF_DEV = 64
E_WIN = 4
CAP = 4
TOKS_PP = 2048
N_PP = 16
N_EP = 32


def block_scale(rng, shape, split, smallest, high):
    def one(axis_at, shards_of):
        heights = jax.random.uniform(jax.random.fold_in(jax.random.fold_in(rng, 6), axis_at), (shards_of,), jnp.float32, smallest / len(split), high / len(split))
        return jnp.repeat(jnp.exp(heights), shape[axis_at] // shards_of).reshape((-1,) + (1,) * (len(shape) - axis_at - 1))

    gain = one(*split[0])
    for cut in split[1:]:
        gain = gain * one(*cut)
    return gain


def deal_out(own_key, own, number, rows, count, top, reach, skew):
    sequence = jax.random.permutation(own_key, count)
    crowded, usual = portions_of(count, rows * top, reach, skew, True), portions_of(count, rows * top, reach, skew, False)
    places = jnp.arange(count)

    def named(sizes, turn):
        used = int((sizes > 0).sum())
        fixed = max(1, used // 4)
        passed = fixed + (places - fixed + turn * (used - fixed)) % max(1, count - fixed)
        return jnp.zeros((count,), jnp.int32).at[sequence[jnp.where(places < fixed, places, passed)]].set(jnp.asarray(sizes, jnp.int32))

    sizes = jnp.where(number % 4 == 0, named(crowded, number // 4), named(usual, number - number // 4 - 1))
    mixed = jax.random.permutation(jax.random.fold_in(own, 3), count)
    giver, taker = mixed[0:count // 2 * 2:2], mixed[1:count // 2 * 2:2]
    room = jnp.minimum(sizes[giver] - 1, reach - sizes[taker]) // 2
    room = jnp.where((giver == sequence[0]) | (taker == sequence[0]) | (sizes[taker] == 0), 0, jnp.maximum(room, 0))
    passed = jax.random.randint(jax.random.fold_in(own, 4), (count // 2,), 0, 1 << 20) % (room + 1)
    sizes = sizes.at[giver].add(-passed).at[taker].add(passed)
    items = jnp.searchsorted(jnp.cumsum(sizes), jnp.arange(rows * top), side="right").astype(jnp.int32)
    table = items.reshape(top, rows).T
    table = table[jax.random.permutation(jax.random.fold_in(own, 1), rows)]
    turn = jax.random.randint(jax.random.fold_in(own, 2), (rows, 1), 0, top)
    return jnp.take_along_axis(table, (jnp.arange(top)[None, :] + turn) % top, axis=1)


def portions_of(amount, total, most, skew, full):
    portions = [(1 << 20) // math.isqrt(grade ** skew) + 1 for grade in range(1, amount + 1)]
    largest = most if full else min(most, max(-(-total // amount), total * portions[0] // sum(portions)))
    least = 1 if total - largest >= amount - 1 else 0
    holding, spare = [largest] + [least] * (amount - 1), total - largest - least * (amount - 1)
    while spare > 0:
        movable = [i for i in range(1, amount) if holding[i] < largest] or [i for i in range(1, amount) if holding[i] < most]
        mass, remaining = sum([portions[i] for i in movable]), spare
        for i in movable:
            extra = min(most - holding[i], max(1, remaining * portions[i] // mass), spare)
            holding[i] = holding[i] + extra
            spare = spare - extra
    return np.array(holding)


def bell_draw(key, extent, spread, most, split=(), held_as=jnp.bfloat16):
    factor_of = block_scale(key, extent, split, -0.22, 0.18) if split else 1.0
    result = jax.random.normal(key, extent, jnp.float32) * spread * factor_of
    return jnp.minimum(jnp.maximum(result, -most), most).astype(held_as)


def setup_inputs(seed: int = 0) -> dict:
    keys = jax.random.split(jax.random.key(seed), 10)
    rising_state = bell_draw(keys[0], (N_PP, TOKS_PP, D), 1.0, 6.0, ((0, 16), (1, 32)))
    falling_state = bell_draw(keys[1], (N_PP, TOKS_PP, D), 1.0, 6.0, ((0, 16), (1, 32)))
    rising_ids_keys = jax.random.split(jax.random.fold_in(keys[2], 1), STEPS * N_PP * TOKS_PP // HALF_DEV)
    rising_ids_turns = jax.random.permutation(jax.random.fold_in(keys[2], 3), STEPS * N_PP * TOKS_PP // HALF_DEV)
    rising_ids = jax.vmap(lambda own, number: deal_out(jax.random.fold_in(keys[2], 2), own, number, HALF_DEV, EXPERTS, TOP, CAP, 1))(rising_ids_keys, rising_ids_turns).reshape((STEPS, N_PP, TOKS_PP, TOP))
    falling_ids_keys = jax.random.split(jax.random.fold_in(keys[3], 1), STEPS * N_PP * TOKS_PP // HALF_DEV)
    falling_ids_turns = jax.random.permutation(jax.random.fold_in(keys[3], 3), STEPS * N_PP * TOKS_PP // HALF_DEV)
    falling_ids = jax.vmap(lambda own, number: deal_out(jax.random.fold_in(keys[3], 2), own, number, HALF_DEV, EXPERTS, TOP, CAP, 1))(falling_ids_keys, falling_ids_turns).reshape((STEPS, N_PP, TOKS_PP, TOP))
    norm_gain = jnp.clip(1.0 + 0.18 * jax.random.normal(keys[4], (N_PP, D), jnp.float32), 0.1, 1.9)
    router = bell_draw(keys[5], (N_PP, EXPERTS, D), D ** -0.5, 0.09375, ((0, 16), (1, 32)))
    w_gate = bell_draw(keys[6], (N_PP, D, E_WIN * EXP_WIDTH), D ** -0.5, 0.09375, ((0, 16), (2, 32)))
    w_up = bell_draw(keys[7], (N_PP, D, E_WIN * EXP_WIDTH), D ** -0.5, 0.09375, ((0, 16), (2, 32)))
    w_down = bell_draw(keys[8], (N_PP, E_WIN * EXP_WIDTH, D), EXP_WIDTH ** -0.5, 0.1875, ((0, 16), (1, 32)))
    return {"rising_state": rising_state, "falling_state": falling_state, "rising_ids": rising_ids, "falling_ids": falling_ids, "norm_gain": norm_gain, "router": router, "w_gate": w_gate, "w_up": w_up, "w_down": w_down}


route_scale = 2.5
norm_eps = 1e-06

def rms_normed(states, norm_gain):
    values = states.astype(jnp.float32)
    inverse = lax.rsqrt(lax.optimization_barrier(jnp.mean(values * values, axis=-1, keepdims=True)) + norm_eps)
    return (values * inverse * norm_gain).astype(jnp.bfloat16)

def gate_values(normed, router, expert_ids):
    logits = jnp.dot(normed, router.T, preferred_element_type=jnp.float32)
    columns = jnp.arange(EXPERTS, dtype=jnp.int32)
    picked = lax.optimization_barrier(jnp.sum(jnp.where(expert_ids[:, :, None] == columns[None, None, :], logits[:, None, :], jnp.zeros((), jnp.float32)), axis=-1))
    affinity = jax.nn.sigmoid(picked)
    return route_scale * affinity / lax.optimization_barrier(jnp.sum(affinity, axis=-1, keepdims=True))

def one_layer(states, expert_ids, norm_gain, router, w_gate, w_up, w_down):
    normed = rms_normed(states, norm_gain)
    gate_weights = gate_values(normed, router, expert_ids)
    per_source = expert_ids.reshape(N_EP, HALF_DEV * TOP)
    window = jnp.arange(E_WIN, dtype=jnp.int32)
    onehot = (per_source[:, :, None] == window[None, None, :]).astype(jnp.int32)
    earlier = jnp.cumsum(onehot, axis=1) - onehot
    slot_index = lax.optimization_barrier(jnp.sum(onehot * earlier, axis=-1))
    source = jnp.arange(N_EP, dtype=jnp.int32)[:, None]
    spare_slot = E_WIN * N_EP * CAP
    target = jnp.where(per_source < E_WIN, (per_source * N_EP + source) * CAP + slot_index, spare_slot).astype(jnp.int32)
    token_index = jnp.repeat(jnp.arange(TOKS_PP, dtype=jnp.int32), TOP)
    row_table = jnp.zeros((spare_slot + 1,), jnp.int32).at[target.reshape(-1)].set(token_index)
    filled = jnp.zeros((spare_slot + 1,), jnp.int32).at[target.reshape(-1)].set(1)
    token_rows = jnp.where(filled[:spare_slot, None] > 0, normed[row_table[:spare_slot]], jnp.zeros((), jnp.bfloat16))
    token_rows = token_rows.reshape(E_WIN, N_EP * CAP, D)
    gate_cols = w_gate.reshape(D, E_WIN, EXP_WIDTH).transpose(1, 0, 2)
    up_cols = w_up.reshape(D, E_WIN, EXP_WIDTH).transpose(1, 0, 2)
    down_rows = w_down.reshape(E_WIN, SPLIT, EXP_WIDTH // SPLIT, D)

    def one_expert(operands):
        rows_e, gate_e, up_e, down_e = operands
        gate_out = jnp.dot(rows_e, gate_e, preferred_element_type=jnp.float32)
        up_out = jnp.dot(rows_e, up_e, preferred_element_type=jnp.float32)
        hidden = (jax.nn.silu(gate_out) * up_out).astype(jnp.bfloat16)
        hidden = hidden.reshape(N_EP * CAP, SPLIT, EXP_WIDTH // SPLIT)
        pieces = jnp.einsum('rsf,sfd->rsd', hidden.astype(jnp.float32), down_e.astype(jnp.float32)).astype(jnp.bfloat16)
        pieces = lax.optimization_barrier(pieces)
        return lax.optimization_barrier(jnp.sum(pieces.astype(jnp.float32), axis=1))
    results = lax.map(one_expert, (token_rows, gate_cols, up_cols, down_rows))
    expert_out = jnp.concatenate([results.reshape(spare_slot, D), jnp.zeros((1, D), jnp.float32)], axis=0)
    target_tok = target.reshape(TOKS_PP, TOP)
    combined = jnp.zeros((TOKS_PP, D), jnp.float32)
    for column in range(TOP):
        combined = combined + gate_weights[:, column, None] * expert_out[target_tok[:, column]]
    return (states.astype(jnp.float32) + combined).astype(jnp.bfloat16)

def apply_layers(states, expert_ids, norm_gain, router, w_gate, w_up, w_down):

    def layer_of(operands):
        return one_layer(*operands)
    return lax.map(layer_of, (states, expert_ids, norm_gain, router, w_gate, w_up, w_down))

def reference(rising_state, falling_state, rising_ids, falling_ids, norm_gain, router, w_gate, w_up, w_down):
    rising = rising_state
    falling = falling_state
    for step_index in range(STEPS):
        rising = apply_layers(rising, rising_ids[step_index], norm_gain, router, w_gate, w_up, w_down)
        falling = apply_layers(falling, falling_ids[step_index], norm_gain, router, w_gate, w_up, w_down)
        rising = jnp.roll(rising, 1, axis=0)
        falling = jnp.roll(falling, -1, axis=0)
    return (rising, falling)
```

```python
import jax
import jax.numpy as jnp
from jax import lax
from jax.experimental import pallas as pl
from jax.experimental.pallas import tpu as pltpu
from jax.sharding import PartitionSpec as P

MESH = pl.DeviceIdType.MESH
F32 = jnp.float32
BF16 = jnp.bfloat16

STEPS = 3
TOP = 8
CAP = 4
N_PP = 16
N_Y = 8
N_Q = 4
TOKS = 64
D = 3584
QW = D // N_Q
ROWS = N_Q * TOKS
UNIT = N_Q * CAP
HID = 128
EXPERTS = 256
HALF = D // 2

route_scale = 2.5
norm_eps = 1e-06


def iota(shape, dim):
    return lax.broadcasted_iota(jnp.int32, shape, dim)


def dot(a, b):
    return jnp.dot(a, b, preferred_element_type=F32)


def dot_t(a, b):
    return lax.dot_general(a, b, (((1,), (1,)), ((), ())), preferred_element_type=F32)


def one_hot(condition):
    return jnp.where(condition, 1.0, 0.0).astype(BF16)


def kernel(
    xr_in, xf_in, idr_in, idf_in, gain, router, wg_in, wu_in, wd_in,
    outr, outf,
    x, ids, normed, packed, zr, rrecv, osend, frecv, ssend, srecv, gsend, grecv,
    ubuf, obuf, acc, wgu, wd, perm, perm_t, rown, rgath, rall,
    sem_in, sem_w, ws_s, ws_r, rt_s, rt_r,
    ya_s, ya_r, yb_s, yb_r, ret_s, ret_r, z_s, z_r, x_s, x_r, s_s, s_r, g_s, g_r,
):
    pp, ep = lax.axis_index("pp"), lax.axis_index("ep")
    zh, y, c = ep // 16, (ep // 2) % N_Y, ep % 2
    oz = 1 - zh

    def at(rank, z, row, core):
        return {"pp": rank, "ep": z * 16 + row * 2 + core}

    def copy(src, dst, send, recv, to):
        return pltpu.make_async_remote_copy(
            src_ref=src, dst_ref=dst, send_sem=send, recv_sem=recv, device_id=to, device_id_type=MESH
        )

    def row_at(shift):
        return lax.rem(y + shift, N_Y)

    def next_rank(d):
        return lax.rem(pp + 1 - 2 * d + N_PP, N_PP)

    def weight_copies():
        low, high = pl.ds(0, HID), pl.ds(HID, HID)
        to = at(pp, zh, y, 1 - c)
        local = [
            pltpu.make_async_copy(wg_in.at[0], wgu.at[:, pl.ds(0, HID)], sem_w.at[0]),
            pltpu.make_async_copy(wu_in.at[0], wgu.at[:, pl.ds(2 * HID, HID)], sem_w.at[1]),
            pltpu.make_async_copy(wd_in.at[0], wd.at[low], sem_w.at[2]),
        ]
        remote = [
            copy(wg_in.at[0], wgu.at[:, pl.ds(HID, HID)], ws_s.at[0], ws_r.at[0], to),
            copy(wu_in.at[0], wgu.at[:, pl.ds(3 * HID, HID)], ws_s.at[1], ws_r.at[1], to),
            copy(wd_in.at[0], wd.at[high], ws_s.at[2], ws_r.at[2], to),
        ]
        return local, remote

    def router_z():
        return copy(rown, rgath.at[0, y, 1], rt_s.at[0], rt_r.at[0], at(pp, oz, y, c))

    def router_right(k):
        block = rgath.at[0, row_at(N_Y - k)]
        return copy(block, block, rt_s.at[1 + k], rt_r.at[1 + k], at(pp, zh, row_at(1), c))

    def router_left(k):
        block = rgath.at[0, row_at(k)]
        return copy(block, block, rt_s.at[5 + k], rt_r.at[5 + k], at(pp, zh, row_at(N_Y - 1), c))

    def router_core():
        return copy(rgath.at[0], rgath.at[1], rt_s.at[8], rt_r.at[8], at(pp, zh, y, 1 - c))

    def send_z(k):
        return copy(packed.at[k, pl.ds(2 * oz, 2)], zr.at[k], z_s.at[k], z_r.at[k], at(pp, oz, y, c))

    def send_ya(k, shift):
        row = row_at(shift)
        return copy(
            packed.at[k, 2 * zh + row // 4], rrecv.at[k, y, 0],
            ya_s.at[k, shift - 1], ya_r.at[k, shift - 1], at(pp, zh, row, c),
        )

    def send_yb(k, shift):
        row = row_at(shift)
        return copy(
            zr.at[k, row // 4], rrecv.at[k, y, 1],
            yb_s.at[k, shift - 1], yb_r.at[k, shift - 1], at(pp, zh, row, c),
        )

    def send_back(k, shift):
        row = row_at(shift)
        return copy(
            osend.at[k, row], frecv.at[k, y],
            ret_s.at[k, shift - 1], ret_r.at[k, shift - 1], at(pp, zh, row, c),
        )

    def send_x(k, d):
        return copy(x.at[k], x.at[k + 2], x_s.at[k], x_r.at[k], at(next_rank(d), zh, y, c))

    def send_sums(k, d):
        dst = srecv.at[k + 2, pl.ds(2 * zh, 2)]
        return [
            copy(ssend.at[k, 0], dst, s_s.at[k, 0], s_r.at[k, 0], at(next_rank(d), zh, y, c)),
            copy(ssend.at[k, 1], dst, s_s.at[k, 1], s_r.at[k, 1], at(next_rank(d), oz, y, c)),
        ]

    def send_gates(k, d):
        return copy(gsend.at[k], grecv.at[k + 2], g_s.at[k], g_r.at[k], at(next_rank(d), zh, y, c))

    def state_in(source, d):
        return [
            pltpu.make_async_copy(
                source.at[0, :, pl.ds(q * QW, QW)], x.at[d, pl.ds(q * TOKS, TOKS)], sem_in.at[d, q]
            )
            for q in range(N_Q)
        ]

    def state_out(d, target):
        return [
            pltpu.make_async_copy(
                x.at[2 * STEPS + d, pl.ds(q * TOKS, TOKS)], target.at[0, :, pl.ds(q * QW, QW)], sem_in.at[d, q]
            )
            for q in range(N_Q)
        ]

    loads = state_in(xr_in, 0) + state_in(xf_in, 1)
    for load in loads:
        load.start()
    local, remote = weight_copies()
    for w in local:
        w.start()
    barrier = pltpu.get_barrier_semaphore()
    peers = [at(pp, zh, row_at(shift), c) for shift in range(1, N_Y)]
    peers += [at(pp, oz, y, c), at(pp, zh, y, 1 - c)]
    for rank in (next_rank(0), next_rank(1)):
        peers += [at(rank, zh, y, c), at(rank, oz, y, c)]
    for peer in peers:
        pl.semaphore_signal(barrier, inc=1, device_id=peer, device_id_type=MESH)

    for s in range(STEPS):
        ids[2 * s] = idr_in[s, 0]
        ids[2 * s + 1] = idf_in[s, 0]
    for d in range(2):
        srecv[d] = jnp.zeros(srecv.shape[1:], BF16)
        grecv[d] = jnp.zeros(grecv.shape[1:], BF16)
    u, r = iota((ROWS, ROWS), 0), iota((ROWS, ROWS), 1)
    perm[...] = one_hot(
        ((u % 64) // 4 == r // 16) & (u // 64 == (r // 4) % 4) & (u % 4 == r % 4)
    )
    perm_t[...] = one_hot(
        ((r % 64) // 4 == u // 16) & (r // 64 == (u // 4) % 4) & (r % 4 == u % 4)
    )
    own = router[0].astype(F32)
    own = jnp.concatenate([own[:, :HALF], own[:, HALF:]], axis=0).astype(BF16)
    rown[...] = own
    rgath[0, y, 0] = own

    pl.semaphore_wait(barrier, len(peers))
    for w in remote:
        w.start()
    router_z().start()
    for load in loads:
        load.wait()

    lane = iota((TOKS, 128), 1)
    lane_e, lane_q, lane_c = (lane % 64) // UNIT, (lane // CAP) % N_Q, lane % CAP

    def matches(k):
        chosen = ids[k]
        hit = jnp.zeros((TOKS, 128), F32)
        for col in range(TOP):
            hit = hit + jnp.where(chosen[:, col : col + 1] == lane_e, 1.0, 0.0)
        before = one_hot(iota((TOKS, TOKS), 0) > iota((TOKS, TOKS), 1))
        earlier = dot(before, hit.astype(BF16))
        return jnp.where(earlier == lane_c.astype(F32), hit, 0.0)

    def by_quarter(table):
        return jnp.concatenate([jnp.where(lane_q == q, table, 0.0) for q in range(N_Q)], axis=0)

    def receive_state(k):
        gates = by_quarter(grecv[k].astype(F32)).astype(BF16)
        sums = srecv[k].reshape(4 * UNIT, QW)
        acc[...] = dot(gates, jnp.concatenate([sums, sums], axis=0))
        squares = jnp.zeros((TOKS, 1), F32)
        for q in range(N_Q):
            rows = pl.ds(q * TOKS, TOKS)
            now = (x[k, rows].astype(F32) + acc[rows]).astype(BF16)
            x[k, rows] = now
            now = now.astype(F32)
            squares = squares + jnp.sum(now * now, axis=-1, keepdims=True)
        return squares

    def wait_state(k, d):
        send_x(k - 2, d).wait_recv()
        for sums in send_sums(k - 2, d):
            sums.wait_recv()
        send_gates(k - 2, d).wait_recv()

    def dispatch(s, d):
        k = 2 * s + d

        @pl.when(s > 0)
        def _():
            wait_state(k, d)

        squares = receive_state(k)
        inverse = lax.rsqrt(squares * (1.0 / D) + norm_eps)
        for q in range(N_Q):
            rows = pl.ds(q * TOKS, TOKS)
            scaled = x[k, rows].astype(F32) * inverse * gain[:, pl.ds(q * QW, QW)]
            normed[d, rows] = scaled.astype(BF16)
        pick = by_quarter(matches(k)).T[: 4 * UNIT].astype(BF16)
        packed[k] = dot(pick, normed[d]).astype(BF16).reshape(4, UNIT, QW)
        send_z(k).start()
        for shift in range(1, N_Y):
            send_ya(k, shift).start()
        send_x(k, d).start()
        rrecv[k, y, 0] = packed[k, 2 * zh + y // 4]

    def relay(s, d):
        k = 2 * s + d
        send_z(k).wait_recv()
        for shift in range(1, N_Y):
            send_yb(k, shift).start()
        rrecv[k, y, 1] = zr[k, y // 4]

    def gather_router():
        router_z().wait_recv()
        for k in range(4):
            if k:
                router_right(k - 1).wait_recv()
            router_right(k).start()
            if k < 3:
                if k:
                    router_left(k - 1).wait_recv()
                router_left(k).start()
        router_left(2).wait_recv()
        router_right(3).wait_recv()
        router_core().start()
        router_core().wait_recv()
        blocks = rgath[...].reshape(2 * EXPERTS, HALF)
        n, row = iota((EXPERTS, 2 * EXPERTS), 0), iota((EXPERTS, 2 * EXPERTS), 1)
        core, place = (row // 256 + c) % 2, (row // 32) % 8
        z = ((row // 16) % 2 + zh) % 2
        expert = (z * 16 + place * 2 + core) * 8 + row % 8
        for h in range(2):
            pick = one_hot((expert == n) & ((row // 8) % 2 == h))
            for part in range(2):
                cols = pl.ds(part * QW, QW)
                rall[2 * h + part] = dot(pick, rgath[:, :, :, :, cols].reshape(2 * EXPERTS, QW)).astype(BF16)

    def gate_table(s, d):
        k = 2 * s + d
        logits = jnp.zeros((TOKS, EXPERTS), F32)
        for q in range(N_Q):
            logits = logits + dot_t(normed[d, pl.ds(q * TOKS, TOKS)], rall[q])
        affinity = jax.nn.sigmoid(logits)
        chosen = ids[k]
        column = iota((TOKS, EXPERTS), 1)
        named = jnp.zeros((TOKS, EXPERTS), F32)
        for col in range(TOP):
            named = named + jnp.where(chosen[:, col : col + 1] == column, affinity, 0.0)
        total = jnp.sum(named, axis=-1, keepdims=True)
        weights = route_scale * affinity[:, :4] / total
        table = jnp.zeros((TOKS, 128), F32)
        for e in range(4):
            table = jnp.where(lane_e == e, weights[:, e : e + 1], table)
        table = table * matches(k)
        high = table.astype(BF16)
        low = (table - high.astype(F32)).astype(BF16)
        gsend[k] = jnp.where(lane < 64, high.astype(F32), low.astype(F32)).astype(BF16)
        send_gates(k, d).start()

    def experts(s, d):
        k = 2 * s + d
        for shift in range(1, N_Y):
            send_ya(k, shift).wait_recv()
        for shift in range(1, N_Y):
            send_yb(k, shift).wait_recv()
        ubuf[...] = dot(perm[...], rrecv[k].reshape(ROWS, QW)).astype(BF16)
        both = jnp.zeros((TOKS, 4 * HID), F32)
        for q in range(N_Q):
            both = both + dot(ubuf[pl.ds(q * TOKS, TOKS)], wgu[pl.ds(q * QW, QW)])
        gate, up = both[:, : 2 * HID], both[:, 2 * HID :]
        hidden = (gate * jax.nn.sigmoid(gate) * up).astype(BF16)
        for q in range(N_Q):
            obuf[pl.ds(q * TOKS, TOKS)] = dot(hidden, wd[:, pl.ds(q * QW, QW)]).astype(BF16)
        osend[k] = dot(perm_t[...], obuf[...]).astype(BF16).reshape(N_Y, 2, UNIT, QW)
        for shift in range(1, N_Y):
            send_back(k, shift).start()
        frecv[k, y] = osend[k, y]

    def finish(s, d):
        k = 2 * s + d
        for shift in range(1, N_Y):
            send_back(k, shift).wait_recv()
        for zs in range(2):
            for e in range(2):
                total = frecv[k, 4 * e, zs].astype(F32)
                for i in range(1, 4):
                    total = total + frecv[k, 4 * e + i, zs].astype(F32)
                ssend[k, zs, e] = total.astype(BF16)
        for sums in send_sums(k, d):
            sums.start()

    def both(phase, s):
        def one(d, carry):
            phase(s, d)
            return carry

        lax.fori_loop(0, 2, one, 0)

    def step(s, carry):
        both(dispatch, s)
        both(relay, s)

        @pl.when(s == 0)
        def _():
            gather_router()

        both(gate_table, s)

        @pl.when(s == 0)
        def _():
            for w in local:
                w.wait()
            for w in remote:
                w.wait_recv()

        both(experts, s)
        both(finish, s)
        return carry

    lax.fori_loop(0, STEPS, step, 0)

    def last(d, carry):
        k = 2 * STEPS + d
        wait_state(k, d)
        receive_state(k)
        return carry

    lax.fori_loop(0, 2, last, 0)
    stores = state_out(0, outr) + state_out(1, outf)
    for store in stores:
        store.start()

    for w in remote:
        w.wait_send()
    router_z().wait_send()
    for k in range(4):
        router_right(k).wait_send()
    for k in range(3):
        router_left(k).wait_send()
    router_core().wait_send()

    def drain(k, carry):
        d = lax.rem(k, 2)
        send_z(k).wait_send()
        for shift in range(1, N_Y):
            send_ya(k, shift).wait_send()
            send_yb(k, shift).wait_send()
            send_back(k, shift).wait_send()
        send_x(k, d).wait_send()
        for sums in send_sums(k, d):
            sums.wait_send()
        send_gates(k, d).wait_send()
        return carry

    lax.fori_loop(0, 2 * STEPS, drain, 0)
    for store in stores:
        store.wait()


def body(rising, falling, rising_ids, falling_ids, norm_gain, router, w_gate, w_up, w_down):
    K = 2 * STEPS
    dma = pltpu.SemaphoreType.DMA
    any_space, vmem = pl.BlockSpec(memory_space=pl.ANY), pl.BlockSpec(memory_space=pltpu.VMEM)
    buffers = [
        ((K + 2, ROWS, QW), BF16),
        ((K, TOKS, TOP), jnp.int32),
        ((2, ROWS, QW), BF16),
        ((K, 4, UNIT, QW), BF16),
        ((K, 2, UNIT, QW), BF16),
        ((K, N_Y, 2, UNIT, QW), BF16),
        ((K, N_Y, 2, UNIT, QW), BF16),
        ((K, N_Y, 2, UNIT, QW), BF16),
        ((K, 2, 2, UNIT, QW), BF16),
        ((K + 2, 4, UNIT, QW), BF16),
        ((K, TOKS, 128), BF16),
        ((K + 2, TOKS, 128), BF16),
        ((ROWS, QW), BF16),
        ((ROWS, QW), BF16),
        ((ROWS, QW), F32),
        ((D, 4 * HID), BF16),
        ((2 * HID, D), BF16),
        ((ROWS, ROWS), BF16),
        ((ROWS, ROWS), BF16),
        ((16, HALF), BF16),
        ((2, N_Y, 2, 16, HALF), BF16),
        ((N_Q, EXPERTS, QW), BF16),
    ]
    semaphores = [
        (2, N_Q), (3,), (3,), (3,), (9,), (9,),
        (K, 7), (K, 7), (K, 7), (K, 7), (K, 7), (K, 7),
        (K,), (K,), (K,), (K,), (K, 2), (K, 2), (K,), (K,),
    ]
    return pl.pallas_call(
        kernel,
        out_shape=[jax.ShapeDtypeStruct(rising.shape, BF16)] * 2,
        in_specs=[any_space, any_space, vmem, vmem, vmem, vmem, any_space, any_space, any_space],
        out_specs=[any_space, any_space],
        scratch_shapes=[pltpu.VMEM(shape, dtype) for shape, dtype in buffers] + [dma(shape) for shape in semaphores],
        compiler_params=pltpu.CompilerParams(
            collective_id=0, has_side_effects=True, vmem_limit_bytes=56 * 1024 * 1024
        ),
        name="moe_relay",
    )(rising, falling, rising_ids, falling_ids, norm_gain, router, w_gate, w_up, w_down)


def solution(mesh):
    return jax.shard_map(
        body,
        mesh=mesh,
        in_specs=(
            P("pp", "ep", None),
            P("pp", "ep", None),
            P(None, "pp", "ep", None),
            P(None, "pp", "ep", None),
            P("pp", None),
            P("pp", "ep", None),
            P("pp", None, "ep"),
            P("pp", None, "ep"),
            P("pp", "ep", None),
        ),
        out_specs=(P("pp", "ep", None), P("pp", "ep", None)),
        check_vma=False,
    )
```

```python
import jax
import jax.numpy as jnp
from jax import lax
from jax.experimental import pallas as pl
from jax.experimental.pallas import tpu as pltpu
from jax.sharding import PartitionSpec as P

MESH = pl.DeviceIdType.MESH
F32 = jnp.float32
BF16 = jnp.bfloat16

STEPS = 3
TOP = 8
CAP = 4
N_PP = 16
N_Y = 8
N_Q = 4
TOKS = 64
D = 3584
QW = D // N_Q
ROWS = N_Q * TOKS
UNIT = N_Q * CAP
HID = 128
EXPERTS = 256
HALF = D // 2

route_scale = 2.5
norm_eps = 1e-06


def iota(shape, dim):
    return lax.broadcasted_iota(jnp.int32, shape, dim)


def dot(a, b):
    return jnp.dot(a, b, preferred_element_type=F32)


def dot_t(a, b):
    return lax.dot_general(a, b, (((1,), (1,)), ((), ())), preferred_element_type=F32)


def one_hot(condition):
    return jnp.where(condition, 1.0, 0.0).astype(BF16)


def kernel(
    xr_in, xf_in, idr_in, idf_in, gain, router, wg_in, wu_in, wd_in,
    outr, outf,
    x, ids, normed, packed, zr, rrecv, osend, frecv, ssend, srecv, gsend, grecv,
    ubuf, obuf, acc, wgu, wd, perm, perm_t, rown, rgath, rall,
    sem_in, sem_w, ws_s, ws_r, rt_s, rt_r,
    ya_s, ya_r, yb_s, yb_r, ret_s, ret_r, z_s, z_r, x_s, x_r, s_s, s_r, g_s, g_r,
):
    pp, ep = lax.axis_index("pp"), lax.axis_index("ep")
    zh, y, c = ep // 16, (ep // 2) % N_Y, ep % 2
    oz = 1 - zh

    def at(rank, z, row, core):
        return {"pp": rank, "ep": z * 16 + row * 2 + core}

    def copy(src, dst, send, recv, to):
        return pltpu.make_async_remote_copy(
            src_ref=src, dst_ref=dst, send_sem=send, recv_sem=recv, device_id=to, device_id_type=MESH
        )

    def row_at(shift):
        return lax.rem(y + shift, N_Y)

    def next_rank(d):
        return lax.rem(pp + 1 - 2 * d + N_PP, N_PP)

    def weight_copies():
        low, high = pl.ds(0, HID), pl.ds(HID, HID)
        to = at(pp, zh, y, 1 - c)
        local = [
            pltpu.make_async_copy(wg_in.at[0], wgu.at[:, pl.ds(0, HID)], sem_w.at[0]),
            pltpu.make_async_copy(wu_in.at[0], wgu.at[:, pl.ds(2 * HID, HID)], sem_w.at[1]),
            pltpu.make_async_copy(wd_in.at[0], wd.at[low], sem_w.at[2]),
        ]
        remote = [
            copy(wg_in.at[0], wgu.at[:, pl.ds(HID, HID)], ws_s.at[0], ws_r.at[0], to),
            copy(wu_in.at[0], wgu.at[:, pl.ds(3 * HID, HID)], ws_s.at[1], ws_r.at[1], to),
            copy(wd_in.at[0], wd.at[high], ws_s.at[2], ws_r.at[2], to),
        ]
        return local, remote

    def router_z():
        return copy(rown, rgath.at[0, y, 1], rt_s.at[0], rt_r.at[0], at(pp, oz, y, c))

    def router_right(k):
        block = rgath.at[0, row_at(N_Y - k)]
        return copy(block, block, rt_s.at[1 + k], rt_r.at[1 + k], at(pp, zh, row_at(1), c))

    def router_left(k):
        block = rgath.at[0, row_at(k)]
        return copy(block, block, rt_s.at[5 + k], rt_r.at[5 + k], at(pp, zh, row_at(N_Y - 1), c))

    def router_core():
        return copy(rgath.at[0], rgath.at[1], rt_s.at[8], rt_r.at[8], at(pp, zh, y, 1 - c))

    def send_z(k):
        return copy(packed.at[k, pl.ds(2 * oz, 2)], zr.at[k], z_s.at[k], z_r.at[k], at(pp, oz, y, c))

    def send_ya(k, shift):
        row = row_at(shift)
        return copy(
            packed.at[k, 2 * zh + row // 4], rrecv.at[k, y, 0],
            ya_s.at[k, shift - 1], ya_r.at[k, shift - 1], at(pp, zh, row, c),
        )

    def send_yb(k, shift):
        row = row_at(shift)
        return copy(
            zr.at[k, row // 4], rrecv.at[k, y, 1],
            yb_s.at[k, shift - 1], yb_r.at[k, shift - 1], at(pp, zh, row, c),
        )

    def send_back(k, shift):
        row = row_at(shift)
        return copy(
            osend.at[k, row], frecv.at[k, y],
            ret_s.at[k, shift - 1], ret_r.at[k, shift - 1], at(pp, zh, row, c),
        )

    def send_x(k, d):
        return copy(x.at[k], x.at[k + 2], x_s.at[k], x_r.at[k], at(next_rank(d), zh, y, c))

    def send_sums(k, d):
        dst = srecv.at[k + 2, pl.ds(2 * zh, 2)]
        return [
            copy(ssend.at[k, 0], dst, s_s.at[k, 0], s_r.at[k, 0], at(next_rank(d), zh, y, c)),
            copy(ssend.at[k, 1], dst, s_s.at[k, 1], s_r.at[k, 1], at(next_rank(d), oz, y, c)),
        ]

    def send_gates(k, d):
        return copy(gsend.at[k], grecv.at[k + 2], g_s.at[k], g_r.at[k], at(next_rank(d), zh, y, c))

    def state_in(source, d):
        return [
            pltpu.make_async_copy(
                source.at[0, :, pl.ds(q * QW, QW)], x.at[d, pl.ds(q * TOKS, TOKS)], sem_in.at[d, q]
            )
            for q in range(N_Q)
        ]

    def state_out(d, target):
        return [
            pltpu.make_async_copy(
                x.at[2 * STEPS + d, pl.ds(q * TOKS, TOKS)], target.at[0, :, pl.ds(q * QW, QW)], sem_in.at[d, q]
            )
            for q in range(N_Q)
        ]

    loads = state_in(xr_in, 0) + state_in(xf_in, 1)
    for load in loads:
        load.start()
    local, remote = weight_copies()
    for w in local:
        w.start()
    barrier = pltpu.get_barrier_semaphore()
    peers = [at(pp, zh, row_at(shift), c) for shift in range(1, N_Y)]
    peers += [at(pp, oz, y, c), at(pp, zh, y, 1 - c)]
    for rank in (next_rank(0), next_rank(1)):
        peers += [at(rank, zh, y, c), at(rank, oz, y, c)]
    for peer in peers:
        pl.semaphore_signal(barrier, inc=1, device_id=peer, device_id_type=MESH)

    for s in range(STEPS):
        ids[2 * s] = idr_in[s, 0]
        ids[2 * s + 1] = idf_in[s, 0]
    for d in range(2):
        srecv[d] = jnp.zeros(srecv.shape[1:], BF16)
        grecv[d] = jnp.zeros(grecv.shape[1:], BF16)
    u, r = iota((ROWS, ROWS), 0), iota((ROWS, ROWS), 1)
    perm[...] = one_hot(
        ((u % 64) // 4 == r // 16) & (u // 64 == (r // 4) % 4) & (u % 4 == r % 4)
    )
    perm_t[...] = one_hot(
        ((r % 64) // 4 == u // 16) & (r // 64 == (u // 4) % 4) & (r % 4 == u % 4)
    )
    own = router[0].astype(F32)
    own = jnp.concatenate([own[:, :HALF], own[:, HALF:]], axis=0).astype(BF16)
    rown[...] = own
    rgath[0, y, 0] = own

    pl.semaphore_wait(barrier, len(peers))
    for w in remote:
        w.start()
    router_z().start()
    for load in loads:
        load.wait()

    lane = iota((TOKS, 128), 1)
    lane_e, lane_q, lane_c = (lane % 64) // UNIT, (lane // CAP) % N_Q, lane % CAP

    def matches(k):
        chosen = ids[k]
        hit = jnp.zeros((TOKS, 128), F32)
        for col in range(TOP):
            hit = hit + jnp.where(chosen[:, col : col + 1] == lane_e, 1.0, 0.0)
        before = one_hot(iota((TOKS, TOKS), 0) > iota((TOKS, TOKS), 1))
        earlier = dot(before, hit.astype(BF16))
        return jnp.where(earlier == lane_c.astype(F32), hit, 0.0)

    def by_quarter(table):
        return jnp.concatenate([jnp.where(lane_q == q, table, 0.0) for q in range(N_Q)], axis=0)

    def receive_state(k):
        gates = by_quarter(grecv[k].astype(F32)).astype(BF16)
        sums = srecv[k].reshape(4 * UNIT, QW)
        acc[...] = dot(gates, jnp.concatenate([sums, sums], axis=0))
        squares = jnp.zeros((TOKS, 1), F32)
        for q in range(N_Q):
            rows = pl.ds(q * TOKS, TOKS)
            now = (x[k, rows].astype(F32) + acc[rows]).astype(BF16)
            x[k, rows] = now
            now = now.astype(F32)
            squares = squares + jnp.sum(now * now, axis=-1, keepdims=True)
        return squares

    def wait_state(k, d):
        send_x(k - 2, d).wait_recv()
        for sums in send_sums(k - 2, d):
            sums.wait_recv()
        send_gates(k - 2, d).wait_recv()

    def at_start(s, more, action):
        @pl.when((s == 0) & more)
        def _():
            action()

    def dispatch(k, s, d, squares):
        inverse = lax.rsqrt(squares * (1.0 / D) + norm_eps)
        for q in range(N_Q):
            rows = pl.ds(q * TOKS, TOKS)
            scaled = x[k, rows].astype(F32) * inverse * gain[:, pl.ds(q * QW, QW)]
            normed[d, rows] = scaled.astype(BF16)
        pick = by_quarter(matches(k)).T[: 4 * UNIT].astype(BF16)
        packed[k] = dot(pick, normed[d]).astype(BF16).reshape(4, UNIT, QW)
        at_start(s, d == 0, lambda: router_hop(0))
        send_z(k).start()
        for shift in range(1, N_Y):
            send_ya(k, shift).start()
        send_x(k, d).start()
        rrecv[k, y, 0] = packed[k, 2 * zh + y // 4]

    def relay(s, d):
        k = 2 * s + d
        send_z(k).wait_recv()
        for shift in range(1, N_Y):
            send_yb(k, shift).start()
        rrecv[k, y, 1] = zr[k, y // 4]

    def router_hop(k):
        if k == 0:
            router_z().wait_recv()
        else:
            router_right(k - 1).wait_recv()
        if k < 4:
            router_right(k).start()
        if 0 < k < 4:
            router_left(k - 1).wait_recv()
        if k < 3:
            router_left(k).start()

    def order_router():
        router_core().wait_recv()
        n, row = iota((EXPERTS, 2 * EXPERTS), 0), iota((EXPERTS, 2 * EXPERTS), 1)
        core, place = (row // 256 + c) % 2, (row // 32) % 8
        z = ((row // 16) % 2 + zh) % 2
        expert = (z * 16 + place * 2 + core) * 8 + row % 8
        for h in range(2):
            pick = one_hot((expert == n) & ((row // 8) % 2 == h))
            for part in range(2):
                cols = pl.ds(part * QW, QW)
                rall[2 * h + part] = dot(pick, rgath[:, :, :, :, cols].reshape(2 * EXPERTS, QW)).astype(BF16)

    def gate_table(s, d):
        k = 2 * s + d
        logits = jnp.zeros((TOKS, EXPERTS), F32)
        for q in range(N_Q):
            logits = logits + dot_t(normed[d, pl.ds(q * TOKS, TOKS)], rall[q])
        affinity = jax.nn.sigmoid(logits)
        chosen = ids[k]
        column = iota((TOKS, EXPERTS), 1)
        named = jnp.zeros((TOKS, EXPERTS), F32)
        for col in range(TOP):
            named = named + jnp.where(chosen[:, col : col + 1] == column, affinity, 0.0)
        total = jnp.sum(named, axis=-1, keepdims=True)
        weights = route_scale * affinity[:, :4] / total
        table = jnp.zeros((TOKS, 128), F32)
        for e in range(4):
            table = jnp.where(lane_e == e, weights[:, e : e + 1], table)
        table = table * matches(k)
        high = table.astype(BF16)
        low = (table - high.astype(F32)).astype(BF16)
        gsend[k] = jnp.where(lane < 64, high.astype(F32), low.astype(F32)).astype(BF16)
        send_gates(k, d).start()

    def experts(s, d):
        k = 2 * s + d
        for shift in range(1, N_Y):
            send_ya(k, shift).wait_recv()
        for shift in range(1, N_Y):
            send_yb(k, shift).wait_recv()
        ubuf[...] = dot(perm[...], rrecv[k].reshape(ROWS, QW)).astype(BF16)
        both = jnp.zeros((TOKS, 4 * HID), F32)
        for q in range(N_Q):
            both = both + dot(ubuf[pl.ds(q * TOKS, TOKS)], wgu[pl.ds(q * QW, QW)])
        gate, up = both[:, : 2 * HID], both[:, 2 * HID :]
        hidden = (gate * jax.nn.sigmoid(gate) * up).astype(BF16)
        for q in range(N_Q):
            obuf[pl.ds(q * TOKS, TOKS)] = dot(hidden, wd[:, pl.ds(q * QW, QW)]).astype(BF16)
        osend[k] = dot(perm_t[...], obuf[...]).astype(BF16).reshape(N_Y, 2, UNIT, QW)
        for shift in range(1, N_Y):
            send_back(k, shift).start()
        frecv[k, y] = osend[k, y]

    def finish(s, d):
        k = 2 * s + d
        for shift in range(1, N_Y):
            send_back(k, shift).wait_recv()
        for zs in range(2):
            for e in range(2):
                total = frecv[k, 4 * e, zs].astype(F32)
                for i in range(1, 4):
                    total = total + frecv[k, 4 * e + i, zs].astype(F32)
                ssend[k, zs, e] = total.astype(BF16)
        for sums in send_sums(k, d):
            sums.start()

    def results(s, d):
        k = 2 * s + d

        @pl.when(s > 0)
        def _():
            finish(s - 1, d)

        @pl.when((s > 0) & (d == 0))
        def _():
            gate_table(s - 1, 1)

        @pl.when((s < STEPS) & (d == 1))
        def _():
            relay(s, 0)
            at_start(s, True, lambda: router_hop(1))

        @pl.when(s > 0)
        def _():
            wait_state(k, d)

        squares = receive_state(k)

        @pl.when(s < STEPS)
        def _():
            dispatch(k, s, d, squares)

    def mlp(s, d):
        at_start(s, d == 0, wait_weights)
        experts(s, d)

        @pl.when((s == 0) & (d == 0))
        def _():
            router_hop(4)
            router_core().start()

    def wait_weights():
        for w in local:
            w.wait()
        for w in remote:
            w.wait_recv()

    def twice(phase, s):
        def one(d, carry):
            phase(s, d)
            return carry

        lax.fori_loop(0, 2, one, 0)

    def step(s, carry):
        twice(results, s)

        @pl.when(s < STEPS)
        def _():
            at_start(s, True, lambda: router_hop(2))
            relay(s, 1)
            at_start(s, True, lambda: router_hop(3))
            twice(mlp, s)
            at_start(s, True, order_router)
            gate_table(s, 0)

        return carry

    lax.fori_loop(0, STEPS + 1, step, 0)
    stores = state_out(0, outr) + state_out(1, outf)
    for store in stores:
        store.start()

    for w in remote:
        w.wait_send()
    router_z().wait_send()
    for k in range(4):
        router_right(k).wait_send()
    for k in range(3):
        router_left(k).wait_send()
    router_core().wait_send()

    def drain(k, carry):
        d = lax.rem(k, 2)
        send_z(k).wait_send()
        for shift in range(1, N_Y):
            send_ya(k, shift).wait_send()
            send_yb(k, shift).wait_send()
            send_back(k, shift).wait_send()
        send_x(k, d).wait_send()
        for sums in send_sums(k, d):
            sums.wait_send()
        send_gates(k, d).wait_send()
        return carry

    lax.fori_loop(0, 2 * STEPS, drain, 0)
    for store in stores:
        store.wait()


def body(rising, falling, rising_ids, falling_ids, norm_gain, router, w_gate, w_up, w_down):
    K = 2 * STEPS
    dma = pltpu.SemaphoreType.DMA
    any_space, vmem = pl.BlockSpec(memory_space=pl.ANY), pl.BlockSpec(memory_space=pltpu.VMEM)
    buffers = [
        ((K + 2, ROWS, QW), BF16),
        ((K, TOKS, TOP), jnp.int32),
        ((2, ROWS, QW), BF16),
        ((K, 4, UNIT, QW), BF16),
        ((K, 2, UNIT, QW), BF16),
        ((K, N_Y, 2, UNIT, QW), BF16),
        ((K, N_Y, 2, UNIT, QW), BF16),
        ((K, N_Y, 2, UNIT, QW), BF16),
        ((K, 2, 2, UNIT, QW), BF16),
        ((K + 2, 4, UNIT, QW), BF16),
        ((K, TOKS, 128), BF16),
        ((K + 2, TOKS, 128), BF16),
        ((ROWS, QW), BF16),
        ((ROWS, QW), BF16),
        ((ROWS, QW), F32),
        ((D, 4 * HID), BF16),
        ((2 * HID, D), BF16),
        ((ROWS, ROWS), BF16),
        ((ROWS, ROWS), BF16),
        ((16, HALF), BF16),
        ((2, N_Y, 2, 16, HALF), BF16),
        ((N_Q, EXPERTS, QW), BF16),
    ]
    semaphores = [
        (2, N_Q), (3,), (3,), (3,), (9,), (9,),
        (K, 7), (K, 7), (K, 7), (K, 7), (K, 7), (K, 7),
        (K,), (K,), (K,), (K,), (K, 2), (K, 2), (K,), (K,),
    ]
    return pl.pallas_call(
        kernel,
        out_shape=[jax.ShapeDtypeStruct(rising.shape, BF16)] * 2,
        in_specs=[any_space, any_space, vmem, vmem, vmem, vmem, any_space, any_space, any_space],
        out_specs=[any_space, any_space],
        scratch_shapes=[pltpu.VMEM(shape, dtype) for shape, dtype in buffers] + [dma(shape) for shape in semaphores],
        compiler_params=pltpu.CompilerParams(
            collective_id=0, has_side_effects=True, vmem_limit_bytes=56 * 1024 * 1024
        ),
        name="moe_relay",
    )(rising, falling, rising_ids, falling_ids, norm_gain, router, w_gate, w_up, w_down)


def solution(mesh):
    return jax.shard_map(
        body,
        mesh=mesh,
        in_specs=(
            P("pp", "ep", None),
            P("pp", "ep", None),
            P(None, "pp", "ep", None),
            P(None, "pp", "ep", None),
            P("pp", None),
            P("pp", "ep", None),
            P("pp", None, "ep"),
            P("pp", None, "ep"),
            P("pp", "ep", None),
        ),
        out_specs=(P("pp", "ep", None), P("pp", "ep", None)),
        check_vma=False,
    )
```

```python
import jax
import jax.numpy as jnp
from jax import lax
from jax.experimental import pallas as pl
from jax.experimental.pallas import tpu as pltpu
from jax.sharding import PartitionSpec as P

MESH = pl.DeviceIdType.MESH
F32 = jnp.float32
BF16 = jnp.bfloat16

STEPS = 3
TOP = 8
CAP = 4
N_PP = 16
N_Y = 8
N_Q = 4
TOKS = 64
D = 3584
QW = D // N_Q
ROWS = N_Q * TOKS
UNIT = N_Q * CAP
HID = 128
EXPERTS = 256
HALF = D // 2

route_scale = 2.5
norm_eps = 1e-06


def iota(shape, dim):
    return lax.broadcasted_iota(jnp.int32, shape, dim)


def dot(a, b):
    return jnp.dot(a, b, preferred_element_type=F32)


def dot_t(a, b):
    return lax.dot_general(a, b, (((1,), (1,)), ((), ())), preferred_element_type=F32)


def one_hot(condition):
    return jnp.where(condition, 1.0, 0.0).astype(BF16)


def kernel(
    xr_in, xf_in, idr_in, idf_in, gain, router, wg_in, wu_in, wd_in,
    outr, outf,
    x, ids, normed, packed, zr, rrecv, osend, frecv, ssend, srecv, gsend, grecv,
    ubuf, obuf, acc, wgu, wd, perm, perm_t, rown, rgath, rall,
    sem_in, sem_w, ws_s, ws_r, rt_s, rt_r,
    ya_s, ya_r, yb_s, yb_r, ret_s, ret_r, z_s, z_r, x_s, x_r, s_s, s_r, g_s, g_r,
):
    pp, ep = lax.axis_index("pp"), lax.axis_index("ep")
    zh, y, c = ep // 16, (ep // 2) % N_Y, ep % 2
    oz = 1 - zh

    def at(rank, z, row, core):
        return {"pp": rank, "ep": z * 16 + row * 2 + core}

    def copy(src, dst, send, recv, to):
        return pltpu.make_async_remote_copy(
            src_ref=src, dst_ref=dst, send_sem=send, recv_sem=recv, device_id=to, device_id_type=MESH
        )

    def row_at(shift):
        return lax.rem(y + shift, N_Y)

    def next_rank(d):
        return lax.rem(pp + 1 - 2 * d + N_PP, N_PP)

    def weight_copies():
        low, high = pl.ds(0, HID), pl.ds(HID, HID)
        to = at(pp, zh, y, 1 - c)
        local = [
            pltpu.make_async_copy(wg_in.at[0], wgu.at[:, pl.ds(0, HID)], sem_w.at[0]),
            pltpu.make_async_copy(wu_in.at[0], wgu.at[:, pl.ds(2 * HID, HID)], sem_w.at[1]),
            pltpu.make_async_copy(wd_in.at[0], wd.at[low], sem_w.at[2]),
        ]
        remote = [
            copy(wg_in.at[0], wgu.at[:, pl.ds(HID, HID)], ws_s.at[0], ws_r.at[0], to),
            copy(wu_in.at[0], wgu.at[:, pl.ds(3 * HID, HID)], ws_s.at[1], ws_r.at[1], to),
            copy(wd_in.at[0], wd.at[high], ws_s.at[2], ws_r.at[2], to),
        ]
        return local, remote

    def router_pair():
        return copy(rown, rgath.at[y, 0, 0], rt_s.at[9], rt_r.at[9], at(pp, zh, y, 1))

    def router_z():
        return copy(rgath.at[y, 0], rgath.at[y, 1], rt_s.at[0], rt_r.at[0], at(pp, oz, y, 1))

    def router_right(k):
        block = rgath.at[row_at(N_Y - k)]
        return copy(block, block, rt_s.at[1 + k], rt_r.at[1 + k], at(pp, zh, row_at(1), 1))

    def router_left(k):
        block = rgath.at[row_at(k)]
        return copy(block, block, rt_s.at[5 + k], rt_r.at[5 + k], at(pp, zh, row_at(N_Y - 1), 1))

    def router_core():
        return copy(rgath, rgath, rt_s.at[8], rt_r.at[8], at(pp, zh, y, 0))

    def send_z(k):
        return copy(packed.at[k, pl.ds(2 * oz, 2)], zr.at[k], z_s.at[k], z_r.at[k], at(pp, oz, y, c))

    def send_ya(k, shift):
        row = row_at(shift)
        return copy(
            packed.at[k, 2 * zh + row // 4], rrecv.at[k, y, 0],
            ya_s.at[k, shift - 1], ya_r.at[k, shift - 1], at(pp, zh, row, c),
        )

    def send_yb(k, shift):
        row = row_at(shift)
        return copy(
            zr.at[k, row // 4], rrecv.at[k, y, 1],
            yb_s.at[k, shift - 1], yb_r.at[k, shift - 1], at(pp, zh, row, c),
        )

    def send_back(k, shift):
        row = row_at(shift)
        return copy(
            osend.at[k, row], frecv.at[k, y],
            ret_s.at[k, shift - 1], ret_r.at[k, shift - 1], at(pp, zh, row, c),
        )

    def send_x(k, d):
        return copy(x.at[k], x.at[k + 2], x_s.at[k], x_r.at[k], at(next_rank(d), zh, y, c))

    def send_sums(k, d):
        dst = srecv.at[k + 2, pl.ds(2 * zh, 2)]
        return [
            copy(ssend.at[k, 0], dst, s_s.at[k, 0], s_r.at[k, 0], at(next_rank(d), zh, y, c)),
            copy(ssend.at[k, 1], dst, s_s.at[k, 1], s_r.at[k, 1], at(next_rank(d), oz, y, c)),
        ]

    def send_gates(k, d):
        return copy(gsend.at[k], grecv.at[k + 2], g_s.at[k], g_r.at[k], at(next_rank(d), zh, y, c))

    def state_in(source, d):
        return [
            pltpu.make_async_copy(
                source.at[0, :, pl.ds(q * QW, QW)], x.at[d, pl.ds(q * TOKS, TOKS)], sem_in.at[d, q]
            )
            for q in range(N_Q)
        ]

    def state_out(d, target):
        return [
            pltpu.make_async_copy(
                x.at[2 * STEPS + d, pl.ds(q * TOKS, TOKS)], target.at[0, :, pl.ds(q * QW, QW)], sem_in.at[d, q]
            )
            for q in range(N_Q)
        ]

    loads = state_in(xr_in, 0) + state_in(xf_in, 1)
    for load in loads:
        load.start()
    local, remote = weight_copies()
    for w in local:
        w.start()
    barrier = pltpu.get_barrier_semaphore()
    peers = [at(pp, zh, row_at(shift), c) for shift in range(1, N_Y)]
    peers += [at(pp, oz, y, c), at(pp, zh, y, 1 - c)]
    for rank in (next_rank(0), next_rank(1)):
        peers += [at(rank, zh, y, c), at(rank, oz, y, c)]
    for peer in peers:
        pl.semaphore_signal(barrier, inc=1, device_id=peer, device_id_type=MESH)

    for s in range(STEPS):
        ids[2 * s] = idr_in[s, 0].T
        ids[2 * s + 1] = idf_in[s, 0].T
    own = router[0].astype(F32)
    own = jnp.concatenate([own[:, :HALF], own[:, HALF:]], axis=0).astype(BF16)
    rown[...] = own

    @pl.when(c == 1)
    def _():
        rgath[y, 0, 1] = own

    for load in loads[:N_Q]:
        load.wait()

    lane = iota((TOKS, 128), 1)
    lane_e, lane_q, lane_c = (lane % 64) // UNIT, (lane // CAP) % N_Q, lane % CAP

    def matches(k):
        chosen = ids[k]
        hit = jnp.zeros((TOKS, 128), F32)
        for col in range(TOP):
            hit = hit + jnp.where(chosen[:, col : col + 1] == lane_e, 1.0, 0.0)
        before = one_hot(iota((TOKS, TOKS), 0) > iota((TOKS, TOKS), 1))
        earlier = dot(before, hit.astype(BF16))
        return jnp.where(earlier == lane_c.astype(F32), hit, 0.0)

    def by_quarter(table):
        return jnp.concatenate([jnp.where(lane_q == q, table, 0.0) for q in range(N_Q)], axis=0)

    def receive_state(k):
        gates = by_quarter(grecv[k].astype(F32)).astype(BF16)
        sums = srecv[k].reshape(4 * UNIT, QW)
        acc[...] = dot(gates, jnp.concatenate([sums, sums], axis=0))
        squares = jnp.zeros((TOKS, 1), F32)
        for q in range(N_Q):
            rows = pl.ds(q * TOKS, TOKS)
            now = (x[k, rows].astype(F32) + acc[rows]).astype(BF16)
            x[k, rows] = now
            now = now.astype(F32)
            squares = squares + jnp.sum(now * now, axis=-1, keepdims=True)
        return squares

    def first_state(d):
        squares = jnp.zeros((TOKS, 1), F32)
        for q in range(N_Q):
            now = x[d, pl.ds(q * TOKS, TOKS)].astype(F32)
            squares = squares + jnp.sum(now * now, axis=-1, keepdims=True)
        return squares

    def wait_state(k, d):
        send_x(k - 2, d).wait_recv()
        for sums in send_sums(k - 2, d):
            sums.wait_recv()
        send_gates(k - 2, d).wait_recv()

    def at_start(s, more, action):
        @pl.when((s == 0) & more)
        def _():
            action()

    def enter():
        pl.semaphore_wait(barrier, len(peers))

        @pl.when(c == 0)
        def _():
            router_pair().start()

    def constants():
        for w in remote:
            w.start()
        u, r = iota((ROWS, ROWS), 0), iota((ROWS, ROWS), 1)
        perm[...] = one_hot(
            ((u % 64) // 4 == r // 16) & (u // 64 == (r // 4) % 4) & (u % 4 == r % 4)
        )
        perm_t[...] = one_hot(
            ((r % 64) // 4 == u // 16) & (r // 64 == (u // 4) % 4) & (r % 4 == u % 4)
        )

        @pl.when(c == 1)
        def _():
            router_pair().wait_recv()
            router_z().start()

    def dispatch(k, d, squares, first=False):
        inverse = lax.rsqrt(squares * (1.0 / D) + norm_eps)
        for q in range(N_Q):
            rows = pl.ds(q * TOKS, TOKS)
            scaled = x[k, rows].astype(F32) * inverse * gain[:, pl.ds(q * QW, QW)]
            normed[d, rows] = scaled.astype(BF16)
        pick = by_quarter(matches(k)).T[: 4 * UNIT].astype(BF16)
        packed[k] = dot(pick, normed[d]).astype(BF16).reshape(4, UNIT, QW)
        if first:
            enter()
        send_z(k).start()
        for shift in range(1, N_Y):
            send_ya(k, shift).start()
        rrecv[k, y, 0] = packed[k, 2 * zh + y // 4]
        if first:
            constants()

    def relay(s, d):
        k = 2 * s + d
        send_z(k).wait_recv()
        for shift in range(1, N_Y):
            send_yb(k, shift).start()
        rrecv[k, y, 1] = zr[k, y // 4]

    def router_hop(k):
        @pl.when(c == 1)
        def _():
            if k == 0:
                router_z().wait_recv()
            else:
                router_right(k - 1).wait_recv()
            if k < 4:
                router_right(k).start()
            if 0 < k < 4:
                router_left(k - 1).wait_recv()
            if k < 3:
                router_left(k).start()
            if k == 4:
                router_core().start()

    def order_router():
        router_hop(4)

        @pl.when(c == 0)
        def _():
            router_core().wait_recv()

        n, row = iota((EXPERTS, 2 * EXPERTS), 0), iota((EXPERTS, 2 * EXPERTS), 1)
        core, place = (row // 16) % 2, row // 64
        z = ((row // 32) % 2 + zh) % 2
        expert = (z * 16 + place * 2 + core) * 8 + row % 8
        for h in range(2):
            pick = one_hot((expert == n) & ((row // 8) % 2 == h))
            for part in range(2):
                cols = pl.ds(part * QW, QW)
                rall[2 * h + part] = dot(pick, rgath[:, :, :, :, cols].reshape(2 * EXPERTS, QW)).astype(BF16)

    def gate_table(s, d):
        k = 2 * s + d
        logits = jnp.zeros((TOKS, EXPERTS), F32)
        for q in range(N_Q):
            logits = logits + dot_t(normed[d, pl.ds(q * TOKS, TOKS)], rall[q])
        affinity = jax.nn.sigmoid(logits)
        chosen = ids[k]
        column = iota((TOKS, EXPERTS), 1)
        named = jnp.zeros((TOKS, EXPERTS), F32)
        for col in range(TOP):
            named = named + jnp.where(chosen[:, col : col + 1] == column, affinity, 0.0)
        total = jnp.sum(named, axis=-1, keepdims=True)
        weights = route_scale * affinity[:, :4] / total
        table = jnp.zeros((TOKS, 128), F32)
        for e in range(4):
            table = jnp.where(lane_e == e, weights[:, e : e + 1], table)
        table = table * matches(k)
        high = table.astype(BF16)
        low = (table - high.astype(F32)).astype(BF16)
        gsend[k] = jnp.where(lane < 64, high.astype(F32), low.astype(F32)).astype(BF16)
        send_gates(k, d).start()

    def experts(s, d):
        k = 2 * s + d
        for shift in range(1, N_Y):
            send_ya(k, shift).wait_recv()
        for shift in range(1, N_Y):
            send_yb(k, shift).wait_recv()
        ubuf[...] = dot(perm[...], rrecv[k].reshape(ROWS, QW)).astype(BF16)
        both = jnp.zeros((TOKS, 4 * HID), F32)
        for q in range(N_Q):
            both = both + dot(ubuf[pl.ds(q * TOKS, TOKS)], wgu[pl.ds(q * QW, QW)])
        gate, up = both[:, : 2 * HID], both[:, 2 * HID :]
        hidden = (gate * jax.nn.sigmoid(gate) * up).astype(BF16)
        for q in range(N_Q):
            obuf[pl.ds(q * TOKS, TOKS)] = dot(hidden, wd[:, pl.ds(q * QW, QW)]).astype(BF16)
        osend[k] = dot(perm_t[...], obuf[...]).astype(BF16).reshape(N_Y, 2, UNIT, QW)
        for shift in range(1, N_Y):
            send_back(k, shift).start()
        frecv[k, y] = osend[k, y]

    def finish(s, d):
        k = 2 * s + d
        for shift in range(1, N_Y):
            send_back(k, shift).wait_recv()
        for zs in range(2):
            for e in range(2):
                total = frecv[k, 4 * e, zs].astype(F32)
                for i in range(1, 4):
                    total = total + frecv[k, 4 * e + i, zs].astype(F32)
                ssend[k, zs, e] = total.astype(BF16)
        for sums in send_sums(k, d):
            sums.start()

    def results(s, d):
        k = 2 * s + 2 + d
        finish(s, d)

        @pl.when(d == 0)
        def _():
            gate_table(s, 1)

        @pl.when((s < STEPS - 1) & (d == 1))
        def _():
            relay(s + 1, 0)

        wait_state(k, d)
        squares = receive_state(k)

        @pl.when(s < STEPS - 1)
        def _():
            dispatch(k, d, squares)

    def mlp(s, d):
        at_start(s, d == 0, wait_weights)
        experts(s, d)

        at_start(s, d == 0, lambda: router_hop(3))

    def wait_weights():
        for w in local:
            w.wait()
        for w in remote:
            w.wait_recv()

    def twice(phase, s):
        def one(d, carry):
            phase(s, d)
            return carry

        lax.fori_loop(0, 2, one, 0)

    def step(s, carry):
        relay(s, 1)
        send_x(2 * s, 0).start()
        send_x(2 * s + 1, 1).start()
        at_start(s, True, lambda: router_hop(2))
        twice(mlp, s)
        at_start(s, True, order_router)
        gate_table(s, 0)
        twice(results, s)
        return carry

    dispatch(0, 0, first_state(0), first=True)
    router_hop(0)
    relay(0, 0)
    for load in loads[N_Q:]:
        load.wait()
    dispatch(1, 1, first_state(1))
    router_hop(1)
    lax.fori_loop(0, STEPS, step, 0)
    stores = state_out(0, outr) + state_out(1, outf)
    for store in stores:
        store.start()

    for w in remote:
        w.wait_send()

    @pl.when(c == 0)
    def _():
        router_pair().wait_send()

    @pl.when(c == 1)
    def _():
        router_z().wait_send()
        for k in range(4):
            router_right(k).wait_send()
        for k in range(3):
            router_left(k).wait_send()
        router_core().wait_send()

    def drain(k, carry):
        d = lax.rem(k, 2)
        send_z(k).wait_send()
        for shift in range(1, N_Y):
            send_ya(k, shift).wait_send()
            send_yb(k, shift).wait_send()
            send_back(k, shift).wait_send()
        send_x(k, d).wait_send()
        for sums in send_sums(k, d):
            sums.wait_send()
        send_gates(k, d).wait_send()
        return carry

    lax.fori_loop(0, 2 * STEPS, drain, 0)
    for store in stores:
        store.wait()


def body(rising, falling, rising_ids, falling_ids, norm_gain, router, w_gate, w_up, w_down):
    K = 2 * STEPS
    dma = pltpu.SemaphoreType.DMA
    any_space, vmem = pl.BlockSpec(memory_space=pl.ANY), pl.BlockSpec(memory_space=pltpu.VMEM)
    buffers = [
        ((K + 2, ROWS, QW), BF16),
        ((K, TOKS, TOP), jnp.int32),
        ((2, ROWS, QW), BF16),
        ((K, 4, UNIT, QW), BF16),
        ((K, 2, UNIT, QW), BF16),
        ((K, N_Y, 2, UNIT, QW), BF16),
        ((K, N_Y, 2, UNIT, QW), BF16),
        ((K, N_Y, 2, UNIT, QW), BF16),
        ((K, 2, 2, UNIT, QW), BF16),
        ((K + 2, 4, UNIT, QW), BF16),
        ((K, TOKS, 128), BF16),
        ((K + 2, TOKS, 128), BF16),
        ((ROWS, QW), BF16),
        ((ROWS, QW), BF16),
        ((ROWS, QW), F32),
        ((D, 4 * HID), BF16),
        ((2 * HID, D), BF16),
        ((ROWS, ROWS), BF16),
        ((ROWS, ROWS), BF16),
        ((16, HALF), BF16),
        ((N_Y, 2, 2, 16, HALF), BF16),
        ((N_Q, EXPERTS, QW), BF16),
    ]
    semaphores = [
        (2, N_Q), (3,), (3,), (3,), (10,), (10,),
        (K, 7), (K, 7), (K, 7), (K, 7), (K, 7), (K, 7),
        (K,), (K,), (K,), (K,), (K, 2), (K, 2), (K,), (K,),
    ]
    return pl.pallas_call(
        kernel,
        out_shape=[jax.ShapeDtypeStruct(rising.shape, BF16)] * 2,
        in_specs=[any_space, any_space, vmem, vmem, vmem, vmem, any_space, any_space, any_space],
        out_specs=[any_space, any_space],
        scratch_shapes=[pltpu.VMEM(shape, dtype) for shape, dtype in buffers] + [dma(shape) for shape in semaphores],
        compiler_params=pltpu.CompilerParams(
            collective_id=0, has_side_effects=True, vmem_limit_bytes=56 * 1024 * 1024
        ),
        name="moe_relay",
    )(rising, falling, jnp.swapaxes(rising_ids, 2, 3), jnp.swapaxes(falling_ids, 2, 3), norm_gain, router, w_gate, w_up, w_down)


def solution(mesh):
    return jax.shard_map(
        body,
        mesh=mesh,
        in_specs=(
            P("pp", "ep", None),
            P("pp", "ep", None),
            P(None, "pp", "ep", None),
            P(None, "pp", "ep", None),
            P("pp", None),
            P("pp", "ep", None),
            P("pp", None, "ep"),
            P("pp", None, "ep"),
            P("pp", "ep", None),
        ),
        out_specs=(P("pp", "ep", None), P("pp", "ep", None)),
        check_vma=False,
    )
```

```python
import jax
import jax.numpy as jnp
from jax import lax
from jax.experimental import pallas as pl
from jax.experimental.pallas import tpu as pltpu
from jax.sharding import PartitionSpec as P

MESH = pl.DeviceIdType.MESH
F32 = jnp.float32
BF16 = jnp.bfloat16

STEPS = 3
TOP = 8
CAP = 4
N_PP = 16
N_Y = 8
N_Q = 4
TOKS = 64
D = 3584
QW = D // N_Q
ROWS = N_Q * TOKS
UNIT = N_Q * CAP
HID = 128
EXPERTS = 256
HALF = D // 2

route_scale = 2.5
norm_eps = 1e-06


def iota(shape, dim):
    return lax.broadcasted_iota(jnp.int32, shape, dim)


def dot(a, b):
    return jnp.dot(a, b, preferred_element_type=F32)


def dot_t(a, b):
    return lax.dot_general(a, b, (((1,), (1,)), ((), ())), preferred_element_type=F32)


def one_hot(condition):
    return jnp.where(condition, 1.0, 0.0).astype(BF16)


def kernel(
    xr_in, xf_in, idr_in, idf_in, gain, router, wg_in, wu_in, wd_in,
    outr, outf,
    x, ids, normed, packed, zr, rrecv, osend, half, rsend, frecv, ssend, srecv, gsend, grecv,
    ubuf, obuf, acc, wgu, wd, perm, perm_t, rown, rgath, rall,
    sem_in, sem_w, ws_s, ws_r, rt_s, rt_r,
    ya_s, ya_r, yb_s, yb_r, ret_s, ret_r, on_s, on_r, half_s, half_r, z_s, z_r, x_s, x_r, s_s, s_r, g_s, g_r,
):
    pp, ep = lax.axis_index("pp"), lax.axis_index("ep")
    zh, y, c = ep // 16, (ep // 2) % N_Y, ep % 2
    oz = 1 - zh
    side = 2 * (y % 2) - 1
    other = y - side

    def at(rank, z, row, core):
        return {"pp": rank, "ep": z * 16 + row * 2 + core}

    def copy(src, dst, send, recv, to):
        return pltpu.make_async_remote_copy(
            src_ref=src, dst_ref=dst, send_sem=send, recv_sem=recv, device_id=to, device_id_type=MESH
        )

    def row_at(shift):
        return lax.rem(y + shift, N_Y)

    def next_rank(d):
        return lax.rem(pp + 1 - 2 * d + N_PP, N_PP)

    def weight_copies():
        low, high = pl.ds(0, HID), pl.ds(HID, HID)
        to = at(pp, zh, y, 1 - c)
        local = [
            pltpu.make_async_copy(wg_in.at[0], wgu.at[:, pl.ds(0, HID)], sem_w.at[0]),
            pltpu.make_async_copy(wu_in.at[0], wgu.at[:, pl.ds(2 * HID, HID)], sem_w.at[1]),
            pltpu.make_async_copy(wd_in.at[0], wd.at[low], sem_w.at[2]),
        ]
        remote = [
            copy(wg_in.at[0], wgu.at[:, pl.ds(HID, HID)], ws_s.at[0], ws_r.at[0], to),
            copy(wu_in.at[0], wgu.at[:, pl.ds(3 * HID, HID)], ws_s.at[1], ws_r.at[1], to),
            copy(wd_in.at[0], wd.at[high], ws_s.at[2], ws_r.at[2], to),
        ]
        return local, remote

    def router_pair():
        return copy(rown, rgath.at[y, 0, 0], rt_s.at[9], rt_r.at[9], at(pp, zh, y, 1))

    def router_z():
        return copy(rgath.at[y, 0], rgath.at[y, 1], rt_s.at[0], rt_r.at[0], at(pp, oz, y, 1))

    def router_right(k):
        block = rgath.at[row_at(N_Y - k)]
        return copy(block, block, rt_s.at[1 + k], rt_r.at[1 + k], at(pp, zh, row_at(1), 1))

    def router_left(k):
        block = rgath.at[row_at(k)]
        return copy(block, block, rt_s.at[5 + k], rt_r.at[5 + k], at(pp, zh, row_at(N_Y - 1), 1))

    def router_core():
        return copy(rgath, rgath, rt_s.at[8], rt_r.at[8], at(pp, zh, y, 0))

    def send_z(k):
        return copy(packed.at[k, pl.ds(2 * oz, 2)], zr.at[k], z_s.at[k], z_r.at[k], at(pp, oz, y, c))

    def handler(j):
        return row_at(N_Y + (side, -2 * side, 3 * side)[j - 1])

    def handled(j):
        return row_at(N_Y + side * j)

    def send_ya(k, j):
        row = handler(j)
        return copy(
            packed.at[k, 2 * zh + row // 4], rrecv.at[k, y, 0],
            ya_s.at[k, j - 1], ya_r.at[k, j - 1], at(pp, zh, row, c),
        )

    def send_yb(k, j):
        row = handler(j)
        return copy(
            zr.at[k, row // 4], rrecv.at[k, y, 1],
            yb_s.at[k, j - 1], yb_r.at[k, j - 1], at(pp, zh, row, c),
        )

    def send_on(k, j):
        rows = rrecv.at[k, handled(j)]
        return copy(rows, rows, on_s.at[k, j], on_r.at[k, j], at(pp, zh, other, c))

    def send_half(k, j):
        row = lax.rem(other - side * j + N_Y, N_Y)
        return copy(osend.at[k, row], half.at[k, j], half_s.at[k, j], half_r.at[k, j], at(pp, zh, other, c))

    def send_back(k, j):
        return copy(
            rsend.at[k, j - 1], frecv.at[k, y // 2],
            ret_s.at[k, j - 1], ret_r.at[k, j - 1], at(pp, zh, handled(j), c),
        )

    def send_x(k, d):
        return copy(x.at[k], x.at[k + 2], x_s.at[k], x_r.at[k], at(next_rank(d), zh, y, c))

    def send_sums(k, d):
        dst = srecv.at[k + 2, pl.ds(2 * zh, 2)]
        return [
            copy(ssend.at[k, 0], dst, s_s.at[k, 0], s_r.at[k, 0], at(next_rank(d), zh, y, c)),
            copy(ssend.at[k, 1], dst, s_s.at[k, 1], s_r.at[k, 1], at(next_rank(d), oz, y, c)),
        ]

    def send_gates(k, d):
        return copy(gsend.at[k], grecv.at[k + 2], g_s.at[k], g_r.at[k], at(next_rank(d), zh, y, c))

    def state_in(source, d):
        return [
            pltpu.make_async_copy(
                source.at[0, :, pl.ds(q * QW, QW)], x.at[d, pl.ds(q * TOKS, TOKS)], sem_in.at[d, q]
            )
            for q in range(N_Q)
        ]

    def state_out(d, target):
        return [
            pltpu.make_async_copy(
                x.at[2 * STEPS + d, pl.ds(q * TOKS, TOKS)], target.at[0, :, pl.ds(q * QW, QW)], sem_in.at[d, q]
            )
            for q in range(N_Q)
        ]

    loads = state_in(xr_in, 0) + state_in(xf_in, 1)
    for load in loads:
        load.start()
    local, remote = weight_copies()
    for w in local:
        w.start()
    barrier = pltpu.get_barrier_semaphore()
    peers = [at(pp, zh, row_at(shift), c) for shift in (1, 2, 3, 5, 6, 7)]
    peers += [at(pp, oz, y, c), at(pp, zh, y, 1 - c)]
    for rank in (next_rank(0), next_rank(1)):
        peers += [at(rank, zh, y, c), at(rank, oz, y, c)]
    for peer in peers:
        pl.semaphore_signal(barrier, inc=1, device_id=peer, device_id_type=MESH)

    for s in range(STEPS):
        ids[2 * s] = idr_in[s, 0].T
        ids[2 * s + 1] = idf_in[s, 0].T
    own = router[0].astype(F32)
    own = jnp.concatenate([own[:, :HALF], own[:, HALF:]], axis=0).astype(BF16)
    rown[...] = own

    @pl.when(c == 1)
    def _():
        rgath[y, 0, 1] = own

    for load in loads[:N_Q]:
        load.wait()

    lane = iota((TOKS, 128), 1)
    lane_e, lane_q, lane_c = (lane % 64) // UNIT, (lane // CAP) % N_Q, lane % CAP

    def matches(k):
        chosen = ids[k]
        hit = jnp.zeros((TOKS, 128), F32)
        for col in range(TOP):
            hit = hit + jnp.where(chosen[:, col : col + 1] == lane_e, 1.0, 0.0)
        before = one_hot(iota((TOKS, TOKS), 0) > iota((TOKS, TOKS), 1))
        earlier = dot(before, hit.astype(BF16))
        return jnp.where(earlier == lane_c.astype(F32), hit, 0.0)

    def by_quarter(table):
        return jnp.concatenate([jnp.where(lane_q == q, table, 0.0) for q in range(N_Q)], axis=0)

    def receive_state(k):
        gates = by_quarter(grecv[k].astype(F32)).astype(BF16)
        sums = srecv[k].reshape(4 * UNIT, QW)
        acc[...] = dot(gates, jnp.concatenate([sums, sums], axis=0))
        squares = jnp.zeros((TOKS, 1), F32)
        for q in range(N_Q):
            rows = pl.ds(q * TOKS, TOKS)
            now = (x[k, rows].astype(F32) + acc[rows]).astype(BF16)
            x[k, rows] = now
            now = now.astype(F32)
            squares = squares + jnp.sum(now * now, axis=-1, keepdims=True)
        return squares

    def first_state(d):
        squares = jnp.zeros((TOKS, 1), F32)
        for q in range(N_Q):
            now = x[d, pl.ds(q * TOKS, TOKS)].astype(F32)
            squares = squares + jnp.sum(now * now, axis=-1, keepdims=True)
        return squares

    def wait_state(k, d):
        send_x(k - 2, d).wait_recv()
        for sums in send_sums(k - 2, d):
            sums.wait_recv()
        send_gates(k - 2, d).wait_recv()

    def at_start(s, more, action):
        @pl.when((s == 0) & more)
        def _():
            action()

    def enter():
        pl.semaphore_wait(barrier, len(peers))

        @pl.when(c == 0)
        def _():
            router_pair().start()

    def constants():
        for w in remote:
            w.start()
        u, r = iota((ROWS, ROWS), 0), iota((ROWS, ROWS), 1)
        perm[...] = one_hot(
            ((u % 64) // 4 == r // 16) & (u // 64 == (r // 4) % 4) & (u % 4 == r % 4)
        )
        perm_t[...] = one_hot(
            ((r % 64) // 4 == u // 16) & (r // 64 == (u // 4) % 4) & (r % 4 == u % 4)
        )

        @pl.when(c == 1)
        def _():
            router_pair().wait_recv()
            router_z().start()

    def dispatch(k, d, squares, first=False):
        inverse = lax.rsqrt(squares * (1.0 / D) + norm_eps)
        for q in range(N_Q):
            rows = pl.ds(q * TOKS, TOKS)
            scaled = x[k, rows].astype(F32) * inverse * gain[:, pl.ds(q * QW, QW)]
            normed[d, rows] = scaled.astype(BF16)
        pick = by_quarter(matches(k)).T[: 4 * UNIT].astype(BF16)
        packed[k] = dot(pick, normed[d]).astype(BF16).reshape(4, UNIT, QW)
        if first:
            enter()
        send_z(k).start()
        for j in (3, 2, 1):
            send_ya(k, j).start()
        rrecv[k, y, 0] = packed[k, 2 * zh + y // 4]
        if first:
            constants()

    def relay(s, d):
        k = 2 * s + d
        send_z(k).wait_recv()
        for j in (3, 2, 1):
            send_yb(k, j).start()
        rrecv[k, y, 1] = zr[k, y // 4]

    def router_hop(k):
        @pl.when(c == 1)
        def _():
            if k == 0:
                router_z().wait_recv()
            else:
                router_right(k - 1).wait_recv()
            if k < 4:
                router_right(k).start()
            if 0 < k < 4:
                router_left(k - 1).wait_recv()
            if k < 3:
                router_left(k).start()
            if k == 4:
                router_core().start()

    def order_router():
        router_hop(4)

        @pl.when(c == 0)
        def _():
            router_core().wait_recv()

        n, row = iota((EXPERTS, 2 * EXPERTS), 0), iota((EXPERTS, 2 * EXPERTS), 1)
        core, place = (row // 16) % 2, row // 64
        z = ((row // 32) % 2 + zh) % 2
        expert = (z * 16 + place * 2 + core) * 8 + row % 8
        for h in range(2):
            pick = one_hot((expert == n) & ((row // 8) % 2 == h))
            for part in range(2):
                cols = pl.ds(part * QW, QW)
                rall[2 * h + part] = dot(pick, rgath[:, :, :, :, cols].reshape(2 * EXPERTS, QW)).astype(BF16)

    def gate_table(s, d):
        k = 2 * s + d
        logits = jnp.zeros((TOKS, EXPERTS), F32)
        for q in range(N_Q):
            logits = logits + dot_t(normed[d, pl.ds(q * TOKS, TOKS)], rall[q])
        affinity = jax.nn.sigmoid(logits)
        chosen = ids[k]
        column = iota((TOKS, EXPERTS), 1)
        named = jnp.zeros((TOKS, EXPERTS), F32)
        for col in range(TOP):
            named = named + jnp.where(chosen[:, col : col + 1] == column, affinity, 0.0)
        total = jnp.sum(named, axis=-1, keepdims=True)
        weights = route_scale * affinity[:, :4] / total
        table = jnp.zeros((TOKS, 128), F32)
        for e in range(4):
            table = jnp.where(lane_e == e, weights[:, e : e + 1], table)
        table = table * matches(k)
        high = table.astype(BF16)
        low = (table - high.astype(F32)).astype(BF16)
        gsend[k] = jnp.where(lane < 64, high.astype(F32), low.astype(F32)).astype(BF16)
        send_gates(k, d).start()

    def experts(s, d):
        k = 2 * s + d
        for j in range(4):
            send_on(k, j).wait_recv()
        ubuf[...] = dot(perm[...], rrecv[k].reshape(ROWS, QW)).astype(BF16)
        both = jnp.zeros((TOKS, 4 * HID), F32)
        for q in range(N_Q):
            both = both + dot(ubuf[pl.ds(q * TOKS, TOKS)], wgu[pl.ds(q * QW, QW)])
        gate, up = both[:, : 2 * HID], both[:, 2 * HID :]
        hidden = (gate * jax.nn.sigmoid(gate) * up).astype(BF16)
        for q in range(N_Q):
            obuf[pl.ds(q * TOKS, TOKS)] = dot(hidden, wd[:, pl.ds(q * QW, QW)]).astype(BF16)
        osend[k] = dot(perm_t[...], obuf[...]).astype(BF16).reshape(N_Y, 2, UNIT, QW)
        for j in (3, 2, 1, 0):
            send_half(k, j).start()

    def forward(s, d):
        k = 2 * s + d
        for j in (1, 2, 3):
            send_ya(k, j).wait_recv()
            send_yb(k, j).wait_recv()
        for j in range(4):
            send_on(k, j).start()

    def reduce_pair(s, d):
        k = 2 * s + d
        for j in (3, 2, 1, 0):
            send_half(k, j).wait_recv()
            total = (osend[k, handled(j)].astype(F32) + half[k, j].astype(F32)).astype(BF16)
            if j:
                rsend[k, j - 1] = total
                send_back(k, j).start()
            else:
                frecv[k, y // 2] = total

    def finish(s, d):
        k = 2 * s + d
        for j in (1, 2, 3):
            send_back(k, j).wait_recv()
        for zs in range(2):
            for e in range(2):
                total = frecv[k, 2 * e, zs].astype(F32) + frecv[k, 2 * e + 1, zs].astype(F32)
                ssend[k, zs, e] = total.astype(BF16)
        for sums in send_sums(k, d):
            sums.start()

    def results(s, d):
        k = 2 * s + 2 + d
        finish(s, d)

        @pl.when(d == 0)
        def _():
            reduce_pair(s, 1)
            at_start(s, True, first_gates)
            gate_table(s, 1)

        @pl.when((s < STEPS - 1) & (d == 1))
        def _():
            relay(s + 1, 0)

        wait_state(k, d)
        squares = receive_state(k)

        @pl.when(s < STEPS - 1)
        def _():
            dispatch(k, d, squares)

    def mlp(s, d):
        forward(s, d)

        @pl.when(d == 1)
        def _():
            pl.when(s > 0)(lambda: gate_table(s, 0))
            reduce_pair(s, 0)

        at_start(s, d == 0, wait_weights)
        experts(s, d)

        at_start(s, d == 0, lambda: router_hop(3))

    def first_gates():
        order_router()
        gate_table(0, 0)

    def wait_weights():
        for w in local:
            w.wait()
        for w in remote:
            w.wait_recv()

    def twice(phase, s):
        def one(d, carry):
            phase(s, d)
            return carry

        lax.fori_loop(0, 2, one, 0)

    def step(s, carry):
        relay(s, 1)
        send_x(2 * s, 0).start()
        send_x(2 * s + 1, 1).start()
        at_start(s, True, lambda: router_hop(2))
        twice(mlp, s)
        twice(results, s)
        return carry

    dispatch(0, 0, first_state(0), first=True)
    router_hop(0)
    relay(0, 0)
    for load in loads[N_Q:]:
        load.wait()
    dispatch(1, 1, first_state(1))
    router_hop(1)
    lax.fori_loop(0, STEPS, step, 0)
    stores = state_out(0, outr) + state_out(1, outf)
    for store in stores:
        store.start()

    for w in remote:
        w.wait_send()

    @pl.when(c == 0)
    def _():
        router_pair().wait_send()

    @pl.when(c == 1)
    def _():
        router_z().wait_send()
        for k in range(4):
            router_right(k).wait_send()
        for k in range(3):
            router_left(k).wait_send()
        router_core().wait_send()

    def drain(k, carry):
        d = lax.rem(k, 2)
        send_z(k).wait_send()
        for j in range(4):
            send_on(k, j).wait_send()
            send_half(k, j).wait_send()
        for j in (1, 2, 3):
            send_ya(k, j).wait_send()
            send_yb(k, j).wait_send()
            send_back(k, j).wait_send()
        send_x(k, d).wait_send()
        for sums in send_sums(k, d):
            sums.wait_send()
        send_gates(k, d).wait_send()
        return carry

    lax.fori_loop(0, 2 * STEPS, drain, 0)
    for store in stores:
        store.wait()


def body(rising, falling, rising_ids, falling_ids, norm_gain, router, w_gate, w_up, w_down):
    K = 2 * STEPS
    dma = pltpu.SemaphoreType.DMA
    any_space, vmem = pl.BlockSpec(memory_space=pl.ANY), pl.BlockSpec(memory_space=pltpu.VMEM)
    buffers = [
        ((K + 2, ROWS, QW), BF16),
        ((K, TOKS, TOP), jnp.int32),
        ((2, ROWS, QW), BF16),
        ((K, 4, UNIT, QW), BF16),
        ((K, 2, UNIT, QW), BF16),
        ((K, N_Y, 2, UNIT, QW), BF16),
        ((K, N_Y, 2, UNIT, QW), BF16),
        ((K, 4, 2, UNIT, QW), BF16),
        ((K, 3, 2, UNIT, QW), BF16),
        ((K, 4, 2, UNIT, QW), BF16),
        ((K, 2, 2, UNIT, QW), BF16),
        ((K + 2, 4, UNIT, QW), BF16),
        ((K, TOKS, 128), BF16),
        ((K + 2, TOKS, 128), BF16),
        ((ROWS, QW), BF16),
        ((ROWS, QW), BF16),
        ((ROWS, QW), F32),
        ((D, 4 * HID), BF16),
        ((2 * HID, D), BF16),
        ((ROWS, ROWS), BF16),
        ((ROWS, ROWS), BF16),
        ((16, HALF), BF16),
        ((N_Y, 2, 2, 16, HALF), BF16),
        ((N_Q, EXPERTS, QW), BF16),
    ]
    semaphores = [
        (2, N_Q), (3,), (3,), (3,), (10,), (10,),
        (K, 3), (K, 3), (K, 3), (K, 3), (K, 3), (K, 3), (K, 4), (K, 4), (K, 4), (K, 4),
        (K,), (K,), (K,), (K,), (K, 2), (K, 2), (K,), (K,),
    ]
    return pl.pallas_call(
        kernel,
        out_shape=[jax.ShapeDtypeStruct(rising.shape, BF16)] * 2,
        in_specs=[any_space, any_space, vmem, vmem, vmem, vmem, any_space, any_space, any_space],
        out_specs=[any_space, any_space],
        scratch_shapes=[pltpu.VMEM(shape, dtype) for shape, dtype in buffers] + [dma(shape) for shape in semaphores],
        compiler_params=pltpu.CompilerParams(
            collective_id=0, has_side_effects=True, vmem_limit_bytes=56 * 1024 * 1024
        ),
        name="moe_relay",
    )(rising, falling, jnp.swapaxes(rising_ids, 2, 3), jnp.swapaxes(falling_ids, 2, 3), norm_gain, router, w_gate, w_up, w_down)


def solution(mesh):
    return jax.shard_map(
        body,
        mesh=mesh,
        in_specs=(
            P("pp", "ep", None),
            P("pp", "ep", None),
            P(None, "pp", "ep", None),
            P(None, "pp", "ep", None),
            P("pp", None),
            P("pp", "ep", None),
            P("pp", None, "ep"),
            P("pp", None, "ep"),
            P("pp", "ep", None),
        ),
        out_specs=(P("pp", "ep", None), P("pp", "ep", None)),
        check_vma=False,
    )
```

```python
import jax
import jax.numpy as jnp
from jax import lax
from jax.experimental import pallas as pl
from jax.experimental.pallas import tpu as pltpu
from jax.sharding import PartitionSpec as P

MESH = pl.DeviceIdType.MESH
F32 = jnp.float32
BF16 = jnp.bfloat16

STEPS = 3
TOP = 8
CAP = 4
N_PP = 16
N_Y = 8
N_Q = 4
TOKS = 64
D = 3584
QW = D // N_Q
ROWS = N_Q * TOKS
FAR_FIRST = (4, 3, 5, 2, 6, 1, 7)
UNIT = N_Q * CAP
HID = 128
EXPERTS = 256
HALF = D // 2

route_scale = 2.5
norm_eps = 1e-06


def iota(shape, dim):
    return lax.broadcasted_iota(jnp.int32, shape, dim)


def dot(a, b):
    return jnp.dot(a, b, preferred_element_type=F32)


def dot_t(a, b):
    return lax.dot_general(a, b, (((1,), (1,)), ((), ())), preferred_element_type=F32)


def one_hot(condition):
    return jnp.where(condition, 1.0, 0.0).astype(BF16)


def kernel(
    xr_in, xf_in, idr_in, idf_in, gain, router, wg_in, wu_in, wd_in,
    outr, outf,
    x, ids, normed, packed, zr, rrecv, osend, frecv, ssend, srecv, gsend, grecv,
    ubuf, obuf, acc, wgu, wd, perm, perm_t, rown, rgath, rall,
    sem_in, sem_w, ws_s, ws_r, rt_s, rt_r,
    ya_s, ya_r, yb_s, yb_r, ret_s, ret_r, z_s, z_r, x_s, x_r, s_s, s_r, g_s, g_r,
):
    pp, ep = lax.axis_index("pp"), lax.axis_index("ep")
    zh, y, c = ep // 16, (ep // 2) % N_Y, ep % 2
    oz = 1 - zh

    def at(rank, z, row, core):
        return {"pp": rank, "ep": z * 16 + row * 2 + core}

    def copy(src, dst, send, recv, to):
        return pltpu.make_async_remote_copy(
            src_ref=src, dst_ref=dst, send_sem=send, recv_sem=recv, device_id=to, device_id_type=MESH
        )

    def row_at(shift):
        return lax.rem(y + shift, N_Y)

    def next_rank(d):
        return lax.rem(pp + 1 - 2 * d + N_PP, N_PP)

    def weight_copies():
        low, high = pl.ds(0, HID), pl.ds(HID, HID)
        to = at(pp, zh, y, 1 - c)
        local = [
            pltpu.make_async_copy(wg_in.at[0], wgu.at[:, pl.ds(0, HID)], sem_w.at[0]),
            pltpu.make_async_copy(wu_in.at[0], wgu.at[:, pl.ds(2 * HID, HID)], sem_w.at[1]),
            pltpu.make_async_copy(wd_in.at[0], wd.at[low], sem_w.at[2]),
        ]
        remote = [
            copy(wg_in.at[0], wgu.at[:, pl.ds(HID, HID)], ws_s.at[0], ws_r.at[0], to),
            copy(wu_in.at[0], wgu.at[:, pl.ds(3 * HID, HID)], ws_s.at[1], ws_r.at[1], to),
            copy(wd_in.at[0], wd.at[high], ws_s.at[2], ws_r.at[2], to),
        ]
        return local, remote

    def router_z():
        return copy(rown, rgath.at[0, y, 1], rt_s.at[0], rt_r.at[0], at(pp, oz, y, c))

    def router_right(k):
        block = rgath.at[0, row_at(N_Y - k)]
        return copy(block, block, rt_s.at[1 + k], rt_r.at[1 + k], at(pp, zh, row_at(1), c))

    def router_left(k):
        block = rgath.at[0, row_at(k)]
        return copy(block, block, rt_s.at[5 + k], rt_r.at[5 + k], at(pp, zh, row_at(N_Y - 1), c))

    def router_core():
        return copy(rgath.at[0], rgath.at[1], rt_s.at[8], rt_r.at[8], at(pp, zh, y, 1 - c))

    def send_z(k):
        return copy(packed.at[k, pl.ds(2 * oz, 2)], zr.at[k], z_s.at[k], z_r.at[k], at(pp, oz, y, c))

    def send_ya(k, shift):
        row = row_at(shift)
        return copy(
            packed.at[k, 2 * zh + row // 4], rrecv.at[k, y, 0],
            ya_s.at[k, shift - 1], ya_r.at[k, shift - 1], at(pp, zh, row, c),
        )

    def send_yb(k, shift):
        row = row_at(shift)
        return copy(
            zr.at[k, row // 4], rrecv.at[k, y, 1],
            yb_s.at[k, shift - 1], yb_r.at[k, shift - 1], at(pp, zh, row, c),
        )

    def send_back(k, shift):
        row = row_at(shift)
        return copy(
            osend.at[k, row], frecv.at[k, y],
            ret_s.at[k, shift - 1], ret_r.at[k, shift - 1], at(pp, zh, row, c),
        )

    def send_x(k, d):
        return copy(x.at[k], x.at[k + 2], x_s.at[k], x_r.at[k], at(next_rank(d), zh, y, c))

    def send_sums(k, d):
        dst = srecv.at[k + 2, pl.ds(2 * zh, 2)]
        return [
            copy(ssend.at[k, 0], dst, s_s.at[k, 0], s_r.at[k, 0], at(next_rank(d), zh, y, c)),
            copy(ssend.at[k, 1], dst, s_s.at[k, 1], s_r.at[k, 1], at(next_rank(d), oz, y, c)),
        ]

    def send_gates(k, d):
        return copy(gsend.at[k], grecv.at[k + 2], g_s.at[k], g_r.at[k], at(next_rank(d), zh, y, c))

    def state_in(source, d):
        return [
            pltpu.make_async_copy(
                source.at[0, :, pl.ds(q * QW, QW)], x.at[d, pl.ds(q * TOKS, TOKS)], sem_in.at[d, q]
            )
            for q in range(N_Q)
        ]

    def state_out(d, target):
        return [
            pltpu.make_async_copy(
                x.at[2 * STEPS + d, pl.ds(q * TOKS, TOKS)], target.at[0, :, pl.ds(q * QW, QW)], sem_in.at[d, q]
            )
            for q in range(N_Q)
        ]

    loads = state_in(xr_in, 0) + state_in(xf_in, 1)
    for load in loads:
        load.start()
    local, remote = weight_copies()
    for w in local:
        w.start()
    barrier = pltpu.get_barrier_semaphore()
    peers = [at(pp, zh, row_at(shift), c) for shift in range(1, N_Y)]
    peers += [at(pp, oz, y, c), at(pp, zh, y, 1 - c)]
    for rank in (next_rank(0), next_rank(1)):
        peers += [at(rank, zh, y, c), at(rank, oz, y, c)]
    for peer in peers:
        pl.semaphore_signal(barrier, inc=1, device_id=peer, device_id_type=MESH)

    for s in range(STEPS):
        ids[2 * s] = idr_in[s, 0].T
        ids[2 * s + 1] = idf_in[s, 0].T
    own = router[0].astype(F32)
    own = jnp.concatenate([own[:, :HALF], own[:, HALF:]], axis=0).astype(BF16)
    rown[...] = own
    rgath[0, y, 0] = own

    for load in loads[:N_Q]:
        load.wait()

    lane = iota((TOKS, 128), 1)
    lane_e, lane_q, lane_c = (lane % 64) // UNIT, (lane // CAP) % N_Q, lane % CAP

    def matches(k):
        chosen = ids[k]
        hit = jnp.zeros((TOKS, 128), F32)
        for col in range(TOP):
            hit = hit + jnp.where(chosen[:, col : col + 1] == lane_e, 1.0, 0.0)
        before = one_hot(iota((TOKS, TOKS), 0) > iota((TOKS, TOKS), 1))
        earlier = dot(before, hit.astype(BF16))
        return jnp.where(earlier == lane_c.astype(F32), hit, 0.0)

    def by_quarter(table):
        return jnp.concatenate([jnp.where(lane_q == q, table, 0.0) for q in range(N_Q)], axis=0)

    def receive_state(k):
        gates = by_quarter(grecv[k].astype(F32)).astype(BF16)
        sums = srecv[k].reshape(4 * UNIT, QW)
        acc[...] = dot(gates, jnp.concatenate([sums, sums], axis=0))
        squares = jnp.zeros((TOKS, 1), F32)
        for q in range(N_Q):
            rows = pl.ds(q * TOKS, TOKS)
            now = (x[k, rows].astype(F32) + acc[rows]).astype(BF16)
            x[k, rows] = now
            now = now.astype(F32)
            squares = squares + jnp.sum(now * now, axis=-1, keepdims=True)
        return squares

    def first_state(d):
        squares = jnp.zeros((TOKS, 1), F32)
        for q in range(N_Q):
            now = x[d, pl.ds(q * TOKS, TOKS)].astype(F32)
            squares = squares + jnp.sum(now * now, axis=-1, keepdims=True)
        return squares

    def wait_state(k, d):
        send_x(k - 2, d).wait_recv()
        for sums in send_sums(k - 2, d):
            sums.wait_recv()
        send_gates(k - 2, d).wait_recv()

    def at_start(s, more, action):
        @pl.when((s == 0) & more)
        def _():
            action()

    def enter():
        pl.semaphore_wait(barrier, len(peers))
        router_z().start()

    def constants():
        for w in remote:
            w.start()
        u, r = iota((ROWS, ROWS), 0), iota((ROWS, ROWS), 1)
        perm[...] = one_hot(
            ((u % 64) // 4 == r // 16) & (u // 64 == (r // 4) % 4) & (u % 4 == r % 4)
        )
        perm_t[...] = one_hot(
            ((r % 64) // 4 == u // 16) & (r // 64 == (u // 4) % 4) & (r % 4 == u % 4)
        )

    def dispatch(k, d, squares, first=False):
        inverse = lax.rsqrt(squares * (1.0 / D) + norm_eps)
        for q in range(N_Q):
            rows = pl.ds(q * TOKS, TOKS)
            scaled = x[k, rows].astype(F32) * inverse * gain[:, pl.ds(q * QW, QW)]
            normed[d, rows] = scaled.astype(BF16)
        pick = by_quarter(matches(k)).T[: 4 * UNIT].astype(BF16)
        packed[k] = dot(pick, normed[d]).astype(BF16).reshape(4, UNIT, QW)
        if first:
            enter()
        send_z(k).start()
        for shift in FAR_FIRST:
            send_ya(k, shift).start()
        rrecv[k, y, 0] = packed[k, 2 * zh + y // 4]
        if first:
            constants()

    def relay(s, d):
        k = 2 * s + d
        send_z(k).wait_recv()
        for shift in FAR_FIRST:
            send_yb(k, shift).start()
        rrecv[k, y, 1] = zr[k, y // 4]

    def router_hop(k):
        if k == 0:
            router_z().wait_recv()
        else:
            router_right(k - 1).wait_recv()
        if k < 4:
            router_right(k).start()
        if 0 < k < 4:
            router_left(k - 1).wait_recv()
        if k < 3:
            router_left(k).start()

    def order_router():
        router_hop(4)
        router_core().start()
        router_core().wait_recv()
        n, row = iota((EXPERTS, 2 * EXPERTS), 0), iota((EXPERTS, 2 * EXPERTS), 1)
        core, place = (row // 256 + c) % 2, (row // 32) % 8
        z = ((row // 16) % 2 + zh) % 2
        expert = (z * 16 + place * 2 + core) * 8 + row % 8
        for h in range(2):
            pick = one_hot((expert == n) & ((row // 8) % 2 == h))
            for part in range(2):
                cols = pl.ds(part * QW, QW)
                rall[2 * h + part] = dot(pick, rgath[:, :, :, :, cols].reshape(2 * EXPERTS, QW)).astype(BF16)

    def gate_table(s, d):
        k = 2 * s + d
        logits = jnp.zeros((TOKS, EXPERTS), F32)
        for q in range(N_Q):
            logits = logits + dot_t(normed[d, pl.ds(q * TOKS, TOKS)], rall[q])
        affinity = jax.nn.sigmoid(logits)
        chosen = ids[k]
        column = iota((TOKS, EXPERTS), 1)
        named = jnp.zeros((TOKS, EXPERTS), F32)
        for col in range(TOP):
            named = named + jnp.where(chosen[:, col : col + 1] == column, affinity, 0.0)
        total = jnp.sum(named, axis=-1, keepdims=True)
        weights = route_scale * affinity[:, :4] / total
        table = jnp.zeros((TOKS, 128), F32)
        for e in range(4):
            table = jnp.where(lane_e == e, weights[:, e : e + 1], table)
        table = table * matches(k)
        high = table.astype(BF16)
        low = (table - high.astype(F32)).astype(BF16)
        gsend[k] = jnp.where(lane < 64, high.astype(F32), low.astype(F32)).astype(BF16)
        send_gates(k, d).start()

    def experts(s, d):
        k = 2 * s + d
        for shift in range(1, N_Y):
            send_ya(k, shift).wait_recv()
        for shift in range(1, N_Y):
            send_yb(k, shift).wait_recv()
        ubuf[...] = dot(perm[...], rrecv[k].reshape(ROWS, QW)).astype(BF16)
        both = jnp.zeros((TOKS, 4 * HID), F32)
        for q in range(N_Q):
            both = both + dot(ubuf[pl.ds(q * TOKS, TOKS)], wgu[pl.ds(q * QW, QW)])
        gate, up = both[:, : 2 * HID], both[:, 2 * HID :]
        hidden = (gate * jax.nn.sigmoid(gate) * up).astype(BF16)
        for q in range(N_Q):
            obuf[pl.ds(q * TOKS, TOKS)] = dot(hidden, wd[:, pl.ds(q * QW, QW)]).astype(BF16)
        osend[k] = dot(perm_t[...], obuf[...]).astype(BF16).reshape(N_Y, 2, UNIT, QW)
        for shift in FAR_FIRST:
            send_back(k, shift).start()
        frecv[k, y] = osend[k, y]

    def finish(s, d):
        k = 2 * s + d
        for shift in range(1, N_Y):
            send_back(k, shift).wait_recv()
        sums = send_sums(k, d)
        for zs in (1, 0):
            for e in range(2):
                total = frecv[k, 4 * e, zs].astype(F32)
                for i in range(1, 4):
                    total = total + frecv[k, 4 * e + i, zs].astype(F32)
                ssend[k, zs, e] = total.astype(BF16)
            sums[zs].start()

    def results(s, d):
        k = 2 * s + 2 + d
        finish(s, d)

        @pl.when(d == 0)
        def _():
            gate_table(s, 1)

        @pl.when((s < STEPS - 1) & (d == 1))
        def _():
            relay(s + 1, 0)

        wait_state(k, d)
        squares = receive_state(k)

        @pl.when(s < STEPS - 1)
        def _():
            dispatch(k, d, squares)

    def mlp(s, d):
        at_start(s, d == 0, wait_weights)
        experts(s, d)

        at_start(s, d == 0, lambda: router_hop(3))

    def wait_weights():
        for w in local:
            w.wait()
        for w in remote:
            w.wait_recv()

    def twice(phase, s):
        def one(d, carry):
            phase(s, d)
            return carry

        lax.fori_loop(0, 2, one, 0)

    def step(s, carry):
        relay(s, 1)
        send_x(2 * s, 0).start()
        send_x(2 * s + 1, 1).start()
        at_start(s, True, lambda: router_hop(2))
        twice(mlp, s)
        at_start(s, True, order_router)
        gate_table(s, 0)
        twice(results, s)
        return carry

    dispatch(0, 0, first_state(0), first=True)
    router_hop(0)
    relay(0, 0)
    for load in loads[N_Q:]:
        load.wait()
    dispatch(1, 1, first_state(1))
    router_hop(1)
    lax.fori_loop(0, STEPS, step, 0)
    stores = state_out(0, outr) + state_out(1, outf)
    for store in stores:
        store.start()

    for w in remote:
        w.wait_send()
    router_z().wait_send()
    for k in range(4):
        router_right(k).wait_send()
    for k in range(3):
        router_left(k).wait_send()
    router_core().wait_send()

    def drain(k, carry):
        d = lax.rem(k, 2)
        send_z(k).wait_send()
        for shift in range(1, N_Y):
            send_ya(k, shift).wait_send()
            send_yb(k, shift).wait_send()
            send_back(k, shift).wait_send()
        send_x(k, d).wait_send()
        for sums in send_sums(k, d):
            sums.wait_send()
        send_gates(k, d).wait_send()
        return carry

    lax.fori_loop(0, 2 * STEPS, drain, 0)
    for store in stores:
        store.wait()


def body(rising, falling, rising_ids, falling_ids, norm_gain, router, w_gate, w_up, w_down):
    K = 2 * STEPS
    dma = pltpu.SemaphoreType.DMA
    any_space, vmem = pl.BlockSpec(memory_space=pl.ANY), pl.BlockSpec(memory_space=pltpu.VMEM)
    buffers = [
        ((K + 2, ROWS, QW), BF16),
        ((K, TOKS, TOP), jnp.int32),
        ((2, ROWS, QW), BF16),
        ((K, 4, UNIT, QW), BF16),
        ((K, 2, UNIT, QW), BF16),
        ((K, N_Y, 2, UNIT, QW), BF16),
        ((K, N_Y, 2, UNIT, QW), BF16),
        ((K, N_Y, 2, UNIT, QW), BF16),
        ((K, 2, 2, UNIT, QW), BF16),
        ((K + 2, 4, UNIT, QW), BF16),
        ((K, TOKS, 128), BF16),
        ((K + 2, TOKS, 128), BF16),
        ((ROWS, QW), BF16),
        ((ROWS, QW), BF16),
        ((ROWS, QW), F32),
        ((D, 4 * HID), BF16),
        ((2 * HID, D), BF16),
        ((ROWS, ROWS), BF16),
        ((ROWS, ROWS), BF16),
        ((16, HALF), BF16),
        ((2, N_Y, 2, 16, HALF), BF16),
        ((N_Q, EXPERTS, QW), BF16),
    ]
    semaphores = [
        (2, N_Q), (3,), (3,), (3,), (9,), (9,),
        (K, 7), (K, 7), (K, 7), (K, 7), (K, 7), (K, 7),
        (K,), (K,), (K,), (K,), (K, 2), (K, 2), (K,), (K,),
    ]
    return pl.pallas_call(
        kernel,
        out_shape=[jax.ShapeDtypeStruct(rising.shape, BF16)] * 2,
        in_specs=[any_space, any_space, vmem, vmem, vmem, vmem, any_space, any_space, any_space],
        out_specs=[any_space, any_space],
        scratch_shapes=[pltpu.VMEM(shape, dtype) for shape, dtype in buffers] + [dma(shape) for shape in semaphores],
        compiler_params=pltpu.CompilerParams(
            collective_id=0, has_side_effects=True, vmem_limit_bytes=56 * 1024 * 1024
        ),
        name="moe_relay",
    )(rising, falling, jnp.swapaxes(rising_ids, 2, 3), jnp.swapaxes(falling_ids, 2, 3), norm_gain, router, w_gate, w_up, w_down)


def solution(mesh):
    return jax.shard_map(
        body,
        mesh=mesh,
        in_specs=(
            P("pp", "ep", None),
            P("pp", "ep", None),
            P(None, "pp", "ep", None),
            P(None, "pp", "ep", None),
            P("pp", None),
            P("pp", "ep", None),
            P("pp", None, "ep"),
            P("pp", None, "ep"),
            P("pp", "ep", None),
        ),
        out_specs=(P("pp", "ep", None), P("pp", "ep", None)),
        check_vma=False,
    )
```

```python
import jax
import jax.numpy as jnp
from jax import lax
from jax.experimental import pallas as pl
from jax.experimental.pallas import tpu as pltpu
from jax.sharding import PartitionSpec as P

MESH = pl.DeviceIdType.MESH
F32 = jnp.float32
BF16 = jnp.bfloat16

STEPS = 3
TOP = 8
CAP = 4
N_PP = 16
N_Y = 8
N_Q = 4
TOKS = 64
D = 3584
QW = D // N_Q
ROWS = N_Q * TOKS
PART = ROWS // 2
FAR_FIRST = (4, 3, 5, 2, 6, 1, 7)
UNIT = N_Q * CAP
HID = 128
EXPERTS = 256
HALF = D // 2

route_scale = 2.5
norm_eps = 1e-06


def iota(shape, dim):
    return lax.broadcasted_iota(jnp.int32, shape, dim)


def dot(a, b):
    return jnp.dot(a, b, preferred_element_type=F32)


def dot_t(a, b):
    return lax.dot_general(a, b, (((1,), (1,)), ((), ())), preferred_element_type=F32)


def one_hot(condition):
    return jnp.where(condition, 1.0, 0.0).astype(BF16)


def kernel(
    xr_in, xf_in, idr_in, idf_in, gain, router, wg_in, wu_in, wd_in,
    outr, outf,
    x, ids, normed, packed, zr, rrecv, osend, frecv, ssend, srecv, gsend, grecv,
    ubuf, obuf, acc, wgu, wd, perm, perm_t, rown, rgath, rall,
    sem_in, sem_w, ws_s, ws_r, rt_s, rt_r,
    y_s, y_r, ret_s, ret_r, z_s, z_r, x_s, x_r, s_s, s_r, g_s, g_r,
):
    pp, ep = lax.axis_index("pp"), lax.axis_index("ep")
    zh, y, c = ep // 16, (ep // 2) % N_Y, ep % 2
    oz = 1 - zh

    def at(rank, z, row, core):
        return {"pp": rank, "ep": z * 16 + row * 2 + core}

    def copy(src, dst, send, recv, to):
        return pltpu.make_async_remote_copy(
            src_ref=src, dst_ref=dst, send_sem=send, recv_sem=recv, device_id=to, device_id_type=MESH
        )

    def row_at(shift):
        return lax.rem(y + shift, N_Y)

    def next_rank(d):
        return lax.rem(pp + 1 - 2 * d + N_PP, N_PP)

    def weight_copies():
        low, high = pl.ds(0, HID), pl.ds(HID, HID)
        to = at(pp, zh, y, 1 - c)
        local = [
            pltpu.make_async_copy(wg_in.at[0], wgu.at[:, pl.ds(0, HID)], sem_w.at[0]),
            pltpu.make_async_copy(wu_in.at[0], wgu.at[:, pl.ds(2 * HID, HID)], sem_w.at[1]),
            pltpu.make_async_copy(wd_in.at[0], wd.at[low], sem_w.at[2]),
        ]
        remote = [
            copy(wg_in.at[0], wgu.at[:, pl.ds(HID, HID)], ws_s.at[0], ws_r.at[0], to),
            copy(wu_in.at[0], wgu.at[:, pl.ds(3 * HID, HID)], ws_s.at[1], ws_r.at[1], to),
            copy(wd_in.at[0], wd.at[high], ws_s.at[2], ws_r.at[2], to),
        ]
        return local, remote

    def router_z():
        return copy(rown, rgath.at[0, y, 1], rt_s.at[0], rt_r.at[0], at(pp, oz, y, c))

    def router_right(k):
        block = rgath.at[0, row_at(N_Y - k)]
        return copy(block, block, rt_s.at[1 + k], rt_r.at[1 + k], at(pp, zh, row_at(1), c))

    def router_left(k):
        block = rgath.at[0, row_at(k)]
        return copy(block, block, rt_s.at[5 + k], rt_r.at[5 + k], at(pp, zh, row_at(N_Y - 1), c))

    def router_core():
        return copy(rgath.at[0], rgath.at[1], rt_s.at[8], rt_r.at[8], at(pp, zh, y, 1 - c))

    def send_z(k):
        return copy(packed.at[k, pl.ds(2 * oz, 2)], zr.at[k], z_s.at[k], z_r.at[k], at(pp, oz, y, c))

    def send_y(k, part, shift, rows):
        return copy(
            rows, rrecv.at[k, y, part],
            y_s.at[k, part, shift - 1], y_r.at[k, part, shift - 1], at(pp, zh, row_at(shift), c),
        )

    def send_ya(k, shift):
        return send_y(k, 0, shift, packed.at[k, 2 * zh + row_at(shift) // 4])

    def send_yb(k, shift):
        return send_y(k, 1, shift, zr.at[k, row_at(shift) // 4])

    def send_back(k, part, shift):
        row = row_at(shift)
        return copy(
            osend.at[k, row, part], frecv.at[k, y, part],
            ret_s.at[k, part, shift - 1], ret_r.at[k, part, shift - 1], at(pp, zh, row, c),
        )

    def send_x(k, d):
        return copy(x.at[k], x.at[k + 2], x_s.at[k], x_r.at[k], at(next_rank(d), zh, y, c))

    def send_sums(k, d):
        dst = srecv.at[k + 2, pl.ds(2 * zh, 2)]
        return [
            copy(ssend.at[k, 0], dst, s_s.at[k, 0], s_r.at[k, 0], at(next_rank(d), zh, y, c)),
            copy(ssend.at[k, 1], dst, s_s.at[k, 1], s_r.at[k, 1], at(next_rank(d), oz, y, c)),
        ]

    def send_gates(k, d):
        return copy(gsend.at[k], grecv.at[k + 2], g_s.at[k], g_r.at[k], at(next_rank(d), zh, y, c))

    def state_in(source, d):
        return [
            pltpu.make_async_copy(
                source.at[0, :, pl.ds(q * QW, QW)], x.at[d, pl.ds(q * TOKS, TOKS)], sem_in.at[d, q]
            )
            for q in range(N_Q)
        ]

    def state_out(d, target):
        return [
            pltpu.make_async_copy(
                x.at[2 * STEPS + d, pl.ds(q * TOKS, TOKS)], target.at[0, :, pl.ds(q * QW, QW)], sem_in.at[d, q]
            )
            for q in range(N_Q)
        ]

    loads = state_in(xr_in, 0) + state_in(xf_in, 1)
    for load in loads:
        load.start()
    local, remote = weight_copies()
    for w in local:
        w.start()
    barrier = pltpu.get_barrier_semaphore()
    peers = [at(pp, zh, row_at(shift), c) for shift in range(1, N_Y)]
    peers += [at(pp, oz, y, c), at(pp, zh, y, 1 - c)]
    for rank in (next_rank(0), next_rank(1)):
        peers += [at(rank, zh, y, c), at(rank, oz, y, c)]
    for peer in peers:
        pl.semaphore_signal(barrier, inc=1, device_id=peer, device_id_type=MESH)

    for s in range(STEPS):
        ids[2 * s] = idr_in[s, 0].T
        ids[2 * s + 1] = idf_in[s, 0].T
    own = router[0].astype(F32)
    own = jnp.concatenate([own[:, :HALF], own[:, HALF:]], axis=0).astype(BF16)
    rown[...] = own
    rgath[0, y, 0] = own

    for load in loads[:N_Q]:
        load.wait()

    lane = iota((TOKS, 128), 1)
    lane_e, lane_q, lane_c = (lane % 64) // UNIT, (lane // CAP) % N_Q, lane % CAP

    def matches(k):
        chosen = ids[k]
        hit = jnp.zeros((TOKS, 128), F32)
        for col in range(TOP):
            hit = hit + jnp.where(chosen[:, col : col + 1] == lane_e, 1.0, 0.0)
        before = one_hot(iota((TOKS, TOKS), 0) > iota((TOKS, TOKS), 1))
        earlier = dot(before, hit.astype(BF16))
        return jnp.where(earlier == lane_c.astype(F32), hit, 0.0)

    def by_quarter(table):
        return jnp.concatenate([jnp.where(lane_q == q, table, 0.0) for q in range(N_Q)], axis=0)

    def receive_state(k):
        gates = by_quarter(grecv[k].astype(F32)).astype(BF16)
        sums = srecv[k].reshape(4 * UNIT, QW)
        acc[...] = dot(gates, jnp.concatenate([sums, sums], axis=0))
        squares = jnp.zeros((TOKS, 1), F32)
        for q in range(N_Q):
            rows = pl.ds(q * TOKS, TOKS)
            now = (x[k, rows].astype(F32) + acc[rows]).astype(BF16)
            x[k, rows] = now
            now = now.astype(F32)
            squares = squares + jnp.sum(now * now, axis=-1, keepdims=True)
        return squares

    def first_state(d):
        squares = jnp.zeros((TOKS, 1), F32)
        for q in range(N_Q):
            now = x[d, pl.ds(q * TOKS, TOKS)].astype(F32)
            squares = squares + jnp.sum(now * now, axis=-1, keepdims=True)
        return squares

    def wait_state(k, d):
        send_x(k - 2, d).wait_recv()
        for sums in send_sums(k - 2, d):
            sums.wait_recv()
        send_gates(k - 2, d).wait_recv()

    def at_start(s, more, action):
        @pl.when((s == 0) & more)
        def _():
            action()

    def enter():
        pl.semaphore_wait(barrier, len(peers))
        router_z().start()

    def constants():
        for w in remote:
            w.start()
        u, r = iota((PART, PART), 0), iota((PART, PART), 1)
        perm[...] = one_hot(
            ((u % 32) // 4 == r // 16) & (u // 32 == (r // 4) % 4) & (u % 4 == r % 4)
        )
        perm_t[...] = one_hot(
            ((r % 32) // 4 == u // 16) & (r // 32 == (u // 4) % 4) & (r % 4 == u % 4)
        )

    def dispatch(k, d, squares, first=False):
        inverse = lax.rsqrt(squares * (1.0 / D) + norm_eps)
        for q in range(N_Q):
            rows = pl.ds(q * TOKS, TOKS)
            scaled = x[k, rows].astype(F32) * inverse * gain[:, pl.ds(q * QW, QW)]
            normed[d, rows] = scaled.astype(BF16)
        pick = by_quarter(matches(k)).T[: 4 * UNIT].astype(BF16)
        packed[k] = dot(pick, normed[d]).astype(BF16).reshape(4, UNIT, QW)
        if first:
            enter()
        send_z(k).start()
        for shift in FAR_FIRST:
            send_ya(k, shift).start()
        rrecv[k, y, 0] = packed[k, 2 * zh + y // 4]
        if first:
            constants()

    def relay(s, d):
        k = 2 * s + d
        send_z(k).wait_recv()
        for shift in FAR_FIRST:
            send_yb(k, shift).start()
        rrecv[k, y, 1] = zr[k, y // 4]

    def router_hop(k):
        if k == 0:
            router_z().wait_recv()
        else:
            router_right(k - 1).wait_recv()
        if k < 4:
            router_right(k).start()
        if 0 < k < 4:
            router_left(k - 1).wait_recv()
        if k < 3:
            router_left(k).start()

    def order_router():
        router_hop(4)
        router_core().start()
        router_core().wait_recv()
        n, row = iota((EXPERTS, 2 * EXPERTS), 0), iota((EXPERTS, 2 * EXPERTS), 1)
        core, place = (row // 256 + c) % 2, (row // 32) % 8
        z = ((row // 16) % 2 + zh) % 2
        expert = (z * 16 + place * 2 + core) * 8 + row % 8
        for h in range(2):
            pick = one_hot((expert == n) & ((row // 8) % 2 == h))
            for part in range(2):
                cols = pl.ds(part * QW, QW)
                rall[2 * h + part] = dot(pick, rgath[:, :, :, :, cols].reshape(2 * EXPERTS, QW)).astype(BF16)

    def gate_table(s, d):
        k = 2 * s + d
        logits = jnp.zeros((TOKS, EXPERTS), F32)
        for q in range(N_Q):
            logits = logits + dot_t(normed[d, pl.ds(q * TOKS, TOKS)], rall[q])
        affinity = jax.nn.sigmoid(logits)
        chosen = ids[k]
        column = iota((TOKS, EXPERTS), 1)
        named = jnp.zeros((TOKS, EXPERTS), F32)
        for col in range(TOP):
            named = named + jnp.where(chosen[:, col : col + 1] == column, affinity, 0.0)
        total = jnp.sum(named, axis=-1, keepdims=True)
        weights = route_scale * affinity[:, :4] / total
        table = jnp.zeros((TOKS, 128), F32)
        for e in range(4):
            table = jnp.where(lane_e == e, weights[:, e : e + 1], table)
        table = table * matches(k)
        high = table.astype(BF16)
        low = (table - high.astype(F32)).astype(BF16)
        gsend[k] = jnp.where(lane < 64, high.astype(F32), low.astype(F32)).astype(BF16)
        send_gates(k, d).start()

    def experts(s, d):
        k = 2 * s + d

        def one(part, carry):
            for shift in range(1, N_Y):
                send_y(k, part, shift, zr.at[k, 0]).wait_recv()
            ubuf[...] = dot(perm[...], rrecv[k, :, part].reshape(PART, QW)).astype(BF16)
            both = jnp.zeros((32, 4 * HID), F32)
            for q in range(N_Q):
                both = both + dot(ubuf[pl.ds(q * 32, 32)], wgu[pl.ds(q * QW, QW)])
            gate, up = both[:, : 2 * HID], both[:, 2 * HID :]
            hidden = (gate * jax.nn.sigmoid(gate) * up).astype(BF16)
            for q in range(N_Q):
                obuf[pl.ds(q * 32, 32)] = dot(hidden, wd[:, pl.ds(q * QW, QW)]).astype(BF16)
            osend[k, :, part] = dot(perm_t[...], obuf[...]).astype(BF16).reshape(N_Y, UNIT, QW)
            for shift in FAR_FIRST:
                send_back(k, part, shift).start()
            frecv[k, y, part] = osend[k, y, part]
            return carry

        lax.fori_loop(0, 2, one, 0)

    def finish(s, d):
        k = 2 * s + d
        sums = send_sums(k, d)
        for zs in range(2):
            for shift in range(1, N_Y):
                send_back(k, zs, shift).wait_recv()
            for e in range(2):
                total = frecv[k, 4 * e, zs].astype(F32)
                for i in range(1, 4):
                    total = total + frecv[k, 4 * e + i, zs].astype(F32)
                ssend[k, zs, e] = total.astype(BF16)
            sums[zs].start()

    def results(s, d):
        k = 2 * s + 2 + d
        finish(s, d)

        @pl.when(d == 0)
        def _():
            gate_table(s, 1)

        @pl.when((s < STEPS - 1) & (d == 1))
        def _():
            relay(s + 1, 0)

        wait_state(k, d)
        squares = receive_state(k)

        @pl.when(s < STEPS - 1)
        def _():
            dispatch(k, d, squares)

    def mlp(s, d):
        at_start(s, d == 0, wait_weights)
        experts(s, d)

        at_start(s, d == 0, lambda: router_hop(3))

    def wait_weights():
        for w in local:
            w.wait()
        for w in remote:
            w.wait_recv()

    def twice(phase, s):
        def one(d, carry):
            phase(s, d)
            return carry

        lax.fori_loop(0, 2, one, 0)

    def step(s, carry):
        relay(s, 1)
        send_x(2 * s, 0).start()
        send_x(2 * s + 1, 1).start()
        at_start(s, True, lambda: router_hop(2))
        twice(mlp, s)
        at_start(s, True, order_router)
        gate_table(s, 0)
        twice(results, s)
        return carry

    dispatch(0, 0, first_state(0), first=True)
    router_hop(0)
    relay(0, 0)
    for load in loads[N_Q:]:
        load.wait()
    dispatch(1, 1, first_state(1))
    router_hop(1)
    lax.fori_loop(0, STEPS, step, 0)
    stores = state_out(0, outr) + state_out(1, outf)
    for store in stores:
        store.start()

    for w in remote:
        w.wait_send()
    router_z().wait_send()
    for k in range(4):
        router_right(k).wait_send()
    for k in range(3):
        router_left(k).wait_send()
    router_core().wait_send()

    def drain(k, carry):
        d = lax.rem(k, 2)
        send_z(k).wait_send()
        for shift in range(1, N_Y):
            send_ya(k, shift).wait_send()
            send_yb(k, shift).wait_send()
            send_back(k, 0, shift).wait_send()
            send_back(k, 1, shift).wait_send()
        send_x(k, d).wait_send()
        for sums in send_sums(k, d):
            sums.wait_send()
        send_gates(k, d).wait_send()
        return carry

    lax.fori_loop(0, 2 * STEPS, drain, 0)
    for store in stores:
        store.wait()


def body(rising, falling, rising_ids, falling_ids, norm_gain, router, w_gate, w_up, w_down):
    K = 2 * STEPS
    dma = pltpu.SemaphoreType.DMA
    any_space, vmem = pl.BlockSpec(memory_space=pl.ANY), pl.BlockSpec(memory_space=pltpu.VMEM)
    buffers = [
        ((K + 2, ROWS, QW), BF16),
        ((K, TOKS, TOP), jnp.int32),
        ((2, ROWS, QW), BF16),
        ((K, 4, UNIT, QW), BF16),
        ((K, 2, UNIT, QW), BF16),
        ((K, N_Y, 2, UNIT, QW), BF16),
        ((K, N_Y, 2, UNIT, QW), BF16),
        ((K, N_Y, 2, UNIT, QW), BF16),
        ((K, 2, 2, UNIT, QW), BF16),
        ((K + 2, 4, UNIT, QW), BF16),
        ((K, TOKS, 128), BF16),
        ((K + 2, TOKS, 128), BF16),
        ((PART, QW), BF16),
        ((PART, QW), BF16),
        ((ROWS, QW), F32),
        ((D, 4 * HID), BF16),
        ((2 * HID, D), BF16),
        ((PART, PART), BF16),
        ((PART, PART), BF16),
        ((16, HALF), BF16),
        ((2, N_Y, 2, 16, HALF), BF16),
        ((N_Q, EXPERTS, QW), BF16),
    ]
    semaphores = [
        (2, N_Q), (3,), (3,), (3,), (9,), (9,),
        (K, 2, 7), (K, 2, 7), (K, 2, 7), (K, 2, 7),
        (K,), (K,), (K,), (K,), (K, 2), (K, 2), (K,), (K,),
    ]
    return pl.pallas_call(
        kernel,
        out_shape=[jax.ShapeDtypeStruct(rising.shape, BF16)] * 2,
        in_specs=[any_space, any_space, vmem, vmem, vmem, vmem, any_space, any_space, any_space],
        out_specs=[any_space, any_space],
        scratch_shapes=[pltpu.VMEM(shape, dtype) for shape, dtype in buffers] + [dma(shape) for shape in semaphores],
        compiler_params=pltpu.CompilerParams(
            collective_id=0, has_side_effects=True, vmem_limit_bytes=56 * 1024 * 1024
        ),
        name="moe_relay",
    )(rising, falling, jnp.swapaxes(rising_ids, 2, 3), jnp.swapaxes(falling_ids, 2, 3), norm_gain, router, w_gate, w_up, w_down)


def solution(mesh):
    return jax.shard_map(
        body,
        mesh=mesh,
        in_specs=(
            P("pp", "ep", None),
            P("pp", "ep", None),
            P(None, "pp", "ep", None),
            P(None, "pp", "ep", None),
            P("pp", None),
            P("pp", "ep", None),
            P("pp", None, "ep"),
            P("pp", None, "ep"),
            P("pp", "ep", None),
        ),
        out_specs=(P("pp", "ep", None), P("pp", "ep", None)),
        check_vma=False,
    )
```

```python
import jax
import jax.numpy as jnp
from jax import lax
from jax.experimental import pallas as pl
from jax.experimental.pallas import tpu as pltpu
from jax.sharding import PartitionSpec as P

MESH = pl.DeviceIdType.MESH
F32 = jnp.float32
BF16 = jnp.bfloat16

STEPS = 3
TOP = 8
CAP = 4
N_PP = 16
N_Y = 8
N_Q = 4
TOKS = 64
D = 3584
QW = D // N_Q
ROWS = N_Q * TOKS
PART = ROWS // 2
FAR_FIRST = (4, 3, 5, 2, 6, 1, 7)
UNIT = N_Q * CAP
HID = 128
EXPERTS = 256
HALF = D // 2

route_scale = 2.5
norm_eps = 1e-06


def iota(shape, dim):
    return lax.broadcasted_iota(jnp.int32, shape, dim)


def dot(a, b):
    return jnp.dot(a, b, preferred_element_type=F32)


def dot_t(a, b):
    return lax.dot_general(a, b, (((1,), (1,)), ((), ())), preferred_element_type=F32)


def one_hot(condition):
    return jnp.where(condition, 1.0, 0.0).astype(BF16)


def kernel(
    xr_in, xf_in, idr_in, idf_in, gain, router, wg_in, wu_in, wd_in,
    outr, outf,
    x, ids, normed, packed, zr, rrecv, osend, frecv, ssend, srecv, gsend, grecv,
    ubuf, obuf, acc, wgu, wd, perm, perm_t, rgath, rall,
    sem_in, sem_w, ws_s, ws_r, rt_s, rt_r,
    y_s, y_r, ret_s, ret_r, z_s, z_r, x_s, x_r, s_s, s_r, g_s, g_r,
):
    pp, ep = lax.axis_index("pp"), lax.axis_index("ep")
    zh, y, c = ep // 16, (ep // 2) % N_Y, ep % 2
    oz = 1 - zh

    def at(rank, z, row, core):
        return {"pp": rank, "ep": z * 16 + row * 2 + core}

    def copy(src, dst, send, recv, to):
        return pltpu.make_async_remote_copy(
            src_ref=src, dst_ref=dst, send_sem=send, recv_sem=recv, device_id=to, device_id_type=MESH
        )

    def row_at(shift):
        return lax.rem(y + shift, N_Y)

    def next_rank(d):
        return lax.rem(pp + 1 - 2 * d + N_PP, N_PP)

    def weight_copies():
        low, high = pl.ds(0, HID), pl.ds(HID, HID)
        to = at(pp, zh, y, 1 - c)
        local = [
            pltpu.make_async_copy(wg_in.at[0], wgu.at[:, pl.ds(0, HID)], sem_w.at[0]),
            pltpu.make_async_copy(wu_in.at[0], wgu.at[:, pl.ds(2 * HID, HID)], sem_w.at[1]),
            pltpu.make_async_copy(wd_in.at[0], wd.at[low], sem_w.at[2]),
        ]
        remote = [
            copy(wg_in.at[0], wgu.at[:, pl.ds(HID, HID)], ws_s.at[0], ws_r.at[0], to),
            copy(wu_in.at[0], wgu.at[:, pl.ds(3 * HID, HID)], ws_s.at[1], ws_r.at[1], to),
            copy(wd_in.at[0], wd.at[high], ws_s.at[2], ws_r.at[2], to),
        ]
        return local, remote

    def router_z(i):
        row = row_at(N_Y - i) if i <= 4 else row_at(i - 4)
        return copy(rgath.at[0, row, 0], rgath.at[0, row, 1], rt_s.at[i], rt_r.at[i], at(pp, oz, y, c))

    def router_right(k):
        block = rgath.at[0, row_at(N_Y - k), 0]
        return copy(block, block, rt_s.at[8 + k], rt_r.at[8 + k], at(pp, zh, row_at(1), c))

    def router_left(k):
        block = rgath.at[0, row_at(k), 0]
        return copy(block, block, rt_s.at[12 + k], rt_r.at[12 + k], at(pp, zh, row_at(N_Y - 1), c))

    def router_core():
        return copy(rgath.at[0], rgath.at[1], rt_s.at[15], rt_r.at[15], at(pp, zh, y, 1 - c))

    def send_z(k):
        return copy(packed.at[k, pl.ds(2 * oz, 2)], zr.at[k], z_s.at[k], z_r.at[k], at(pp, oz, y, c))

    def send_y(k, part, shift, rows):
        return copy(
            rows, rrecv.at[k, y, part],
            y_s.at[k, part, shift - 1], y_r.at[k, part, shift - 1], at(pp, zh, row_at(shift), c),
        )

    def send_ya(k, shift):
        return send_y(k, 0, shift, packed.at[k, 2 * zh + row_at(shift) // 4])

    def send_yb(k, shift):
        return send_y(k, 1, shift, zr.at[k, row_at(shift) // 4])

    def send_back(k, part, shift):
        row = row_at(shift)
        return copy(
            osend.at[k, row, part], frecv.at[k, y, part],
            ret_s.at[k, part, shift - 1], ret_r.at[k, part, shift - 1], at(pp, zh, row, c),
        )

    def send_x(k, d):
        return copy(x.at[k], x.at[k + 2], x_s.at[k], x_r.at[k], at(next_rank(d), zh, y, c))

    def send_sums(k, d):
        dst = srecv.at[k + 2, pl.ds(2 * zh, 2)]
        return [
            copy(ssend.at[k, 0], dst, s_s.at[k, 0], s_r.at[k, 0], at(next_rank(d), zh, y, c)),
            copy(ssend.at[k, 1], dst, s_s.at[k, 1], s_r.at[k, 1], at(next_rank(d), oz, y, c)),
        ]

    def send_gates(k, d):
        return copy(gsend.at[k], grecv.at[k + 2], g_s.at[k], g_r.at[k], at(next_rank(d), zh, y, c))

    def state_in(source, d):
        return [
            pltpu.make_async_copy(
                source.at[0, :, pl.ds(q * QW, QW)], x.at[d, pl.ds(q * TOKS, TOKS)], sem_in.at[d, q]
            )
            for q in range(N_Q)
        ]

    def state_out(d, target):
        return [
            pltpu.make_async_copy(
                x.at[2 * STEPS + d, pl.ds(q * TOKS, TOKS)], target.at[0, :, pl.ds(q * QW, QW)], sem_in.at[d, q]
            )
            for q in range(N_Q)
        ]

    loads = state_in(xr_in, 0) + state_in(xf_in, 1)
    for load in loads:
        load.start()
    local, remote = weight_copies()
    for w in local:
        w.start()
    barrier = pltpu.get_barrier_semaphore()
    peers = [at(pp, zh, row_at(shift), c) for shift in range(1, N_Y)]
    peers += [at(pp, oz, y, c), at(pp, zh, y, 1 - c)]
    for rank in (next_rank(0), next_rank(1)):
        peers += [at(rank, zh, y, c), at(rank, oz, y, c)]
    for peer in peers:
        pl.semaphore_signal(barrier, inc=1, device_id=peer, device_id_type=MESH)

    for s in range(STEPS):
        ids[2 * s] = idr_in[s, 0].T
        ids[2 * s + 1] = idf_in[s, 0].T
    own = router[0].astype(F32)
    own = jnp.concatenate([own[:, :HALF], own[:, HALF:]], axis=0).astype(BF16)
    rgath[0, y, 0] = own

    for load in loads[:N_Q]:
        load.wait()

    lane = iota((TOKS, 128), 1)
    lane_e, lane_q, lane_c = (lane % 64) // UNIT, (lane // CAP) % N_Q, lane % CAP

    def matches(k):
        chosen = ids[k]
        hit = jnp.zeros((TOKS, 128), F32)
        for col in range(TOP):
            hit = hit + jnp.where(chosen[:, col : col + 1] == lane_e, 1.0, 0.0)
        before = one_hot(iota((TOKS, TOKS), 0) > iota((TOKS, TOKS), 1))
        earlier = dot(before, hit.astype(BF16))
        return jnp.where(earlier == lane_c.astype(F32), hit, 0.0)

    def by_quarter(table):
        return jnp.concatenate([jnp.where(lane_q == q, table, 0.0) for q in range(N_Q)], axis=0)

    def receive_state(k):
        gates = by_quarter(grecv[k].astype(F32)).astype(BF16)
        sums = srecv[k].reshape(4 * UNIT, QW)
        acc[...] = dot(gates, jnp.concatenate([sums, sums], axis=0))
        squares = jnp.zeros((TOKS, 1), F32)
        for q in range(N_Q):
            rows = pl.ds(q * TOKS, TOKS)
            now = (x[k, rows].astype(F32) + acc[rows]).astype(BF16)
            x[k, rows] = now
            now = now.astype(F32)
            squares = squares + jnp.sum(now * now, axis=-1, keepdims=True)
        return squares

    def first_state(d):
        squares = jnp.zeros((TOKS, 1), F32)
        for q in range(N_Q):
            now = x[d, pl.ds(q * TOKS, TOKS)].astype(F32)
            squares = squares + jnp.sum(now * now, axis=-1, keepdims=True)
        return squares

    def wait_state(k, d):
        send_x(k - 2, d).wait_recv()
        for sums in send_sums(k - 2, d):
            sums.wait_recv()
        send_gates(k - 2, d).wait_recv()

    def at_start(s, more, action):
        @pl.when((s == 0) & more)
        def _():
            action()

    def enter():
        pl.semaphore_wait(barrier, len(peers))
        router_z(0).start()
        router_hop(0)

    def constants():
        for w in remote:
            w.start()
        u, r = iota((PART, PART), 0), iota((PART, PART), 1)
        perm[...] = one_hot(
            ((u % 32) // 4 == r // 16) & (u // 32 == (r // 4) % 4) & (u % 4 == r % 4)
        )
        perm_t[...] = one_hot(
            ((r % 32) // 4 == u // 16) & (r // 32 == (u // 4) % 4) & (r % 4 == u % 4)
        )

    def dispatch(k, d, squares, first=False):
        inverse = lax.rsqrt(squares * (1.0 / D) + norm_eps)
        for q in range(N_Q):
            rows = pl.ds(q * TOKS, TOKS)
            scaled = x[k, rows].astype(F32) * inverse * gain[:, pl.ds(q * QW, QW)]
            normed[d, rows] = scaled.astype(BF16)
        pick = by_quarter(matches(k)).T[: 4 * UNIT].astype(BF16)
        packed[k] = dot(pick, normed[d]).astype(BF16).reshape(4, UNIT, QW)
        if first:
            enter()
        send_z(k).start()
        for shift in FAR_FIRST:
            send_ya(k, shift).start()
        rrecv[k, y, 0] = packed[k, 2 * zh + y // 4]
        if first:
            constants()

    def relay(s, d):
        k = 2 * s + d
        send_z(k).wait_recv()
        for shift in FAR_FIRST:
            send_yb(k, shift).start()
        rrecv[k, y, 1] = zr[k, y // 4]

    def router_hop(k):
        if k:
            router_right(k - 1).wait_recv()
            router_z(k).start()
        if k < 4:
            router_right(k).start()
        if 0 < k < 4:
            router_left(k - 1).wait_recv()
            router_z(4 + k).start()
        if k < 3:
            router_left(k).start()

    def order_router():
        for i in range(8):
            router_z(i).wait_recv()
        router_core().start()
        router_core().wait_recv()
        n, row = iota((EXPERTS, 2 * EXPERTS), 0), iota((EXPERTS, 2 * EXPERTS), 1)
        core, place = (row // 256 + c) % 2, (row // 32) % 8
        z = ((row // 16) % 2 + zh) % 2
        expert = (z * 16 + place * 2 + core) * 8 + row % 8
        for h in range(2):
            pick = one_hot((expert == n) & ((row // 8) % 2 == h))
            for part in range(2):
                cols = pl.ds(part * QW, QW)
                rall[2 * h + part] = dot(pick, rgath[:, :, :, :, cols].reshape(2 * EXPERTS, QW)).astype(BF16)

    def gate_table(s, d):
        k = 2 * s + d
        logits = jnp.zeros((TOKS, EXPERTS), F32)
        for q in range(N_Q):
            logits = logits + dot_t(normed[d, pl.ds(q * TOKS, TOKS)], rall[q])
        affinity = jax.nn.sigmoid(logits)
        chosen = ids[k]
        column = iota((TOKS, EXPERTS), 1)
        named = jnp.zeros((TOKS, EXPERTS), F32)
        for col in range(TOP):
            named = named + jnp.where(chosen[:, col : col + 1] == column, affinity, 0.0)
        total = jnp.sum(named, axis=-1, keepdims=True)
        weights = route_scale * affinity[:, :4] / total
        table = jnp.zeros((TOKS, 128), F32)
        for e in range(4):
            table = jnp.where(lane_e == e, weights[:, e : e + 1], table)
        table = table * matches(k)
        high = table.astype(BF16)
        low = (table - high.astype(F32)).astype(BF16)
        gsend[k] = jnp.where(lane < 64, high.astype(F32), low.astype(F32)).astype(BF16)
        send_gates(k, d).start()

    def experts(s, d):
        k = 2 * s + d

        def one(part, carry):
            for shift in range(1, N_Y):
                send_y(k, part, shift, zr.at[k, 0]).wait_recv()
            ubuf[...] = dot(perm[...], rrecv[k, :, part].reshape(PART, QW)).astype(BF16)
            both = jnp.zeros((32, 4 * HID), F32)
            for q in range(N_Q):
                both = both + dot(ubuf[pl.ds(q * 32, 32)], wgu[pl.ds(q * QW, QW)])
            gate, up = both[:, : 2 * HID], both[:, 2 * HID :]
            hidden = (gate * jax.nn.sigmoid(gate) * up).astype(BF16)
            for q in range(N_Q):
                obuf[pl.ds(q * 32, 32)] = dot(hidden, wd[:, pl.ds(q * QW, QW)]).astype(BF16)
            osend[k, :, part] = dot(perm_t[...], obuf[...]).astype(BF16).reshape(N_Y, UNIT, QW)
            for shift in FAR_FIRST:
                send_back(k, part, shift).start()
            frecv[k, y, part] = osend[k, y, part]
            return carry

        lax.fori_loop(0, 2, one, 0)

    def finish(s, d):
        k = 2 * s + d
        sums = send_sums(k, d)
        for zs in range(2):
            for shift in range(1, N_Y):
                send_back(k, zs, shift).wait_recv()
            for e in range(2):
                total = frecv[k, 4 * e, zs].astype(F32)
                for i in range(1, 4):
                    total = total + frecv[k, 4 * e + i, zs].astype(F32)
                ssend[k, zs, e] = total.astype(BF16)
            sums[zs].start()

    def results(s, d):
        k = 2 * s + 2 + d
        finish(s, d)

        @pl.when(d == 0)
        def _():
            gate_table(s, 1)

        @pl.when((s < STEPS - 1) & (d == 1))
        def _():
            relay(s + 1, 0)

        wait_state(k, d)
        squares = receive_state(k)

        @pl.when(s < STEPS - 1)
        def _():
            dispatch(k, d, squares)

    def mlp(s, d):
        at_start(s, d == 0, wait_weights)
        experts(s, d)

        at_start(s, d == 0, lambda: router_hop(4))

    def wait_weights():
        for w in local:
            w.wait()
        for w in remote:
            w.wait_recv()

    def twice(phase, s):
        def one(d, carry):
            phase(s, d)
            return carry

        lax.fori_loop(0, 2, one, 0)

    def step(s, carry):
        relay(s, 1)
        send_x(2 * s, 0).start()
        send_x(2 * s + 1, 1).start()
        at_start(s, True, lambda: router_hop(3))
        twice(mlp, s)
        at_start(s, True, order_router)
        gate_table(s, 0)
        twice(results, s)
        return carry

    dispatch(0, 0, first_state(0), first=True)
    router_hop(1)
    relay(0, 0)
    for load in loads[N_Q:]:
        load.wait()
    dispatch(1, 1, first_state(1))
    router_hop(2)
    lax.fori_loop(0, STEPS, step, 0)
    stores = state_out(0, outr) + state_out(1, outf)
    for store in stores:
        store.start()

    for w in remote:
        w.wait_send()
    for i in range(8):
        router_z(i).wait_send()
    for k in range(4):
        router_right(k).wait_send()
    for k in range(3):
        router_left(k).wait_send()
    router_core().wait_send()

    def drain(k, carry):
        d = lax.rem(k, 2)
        send_z(k).wait_send()
        for shift in range(1, N_Y):
            send_ya(k, shift).wait_send()
            send_yb(k, shift).wait_send()
            send_back(k, 0, shift).wait_send()
            send_back(k, 1, shift).wait_send()
        send_x(k, d).wait_send()
        for sums in send_sums(k, d):
            sums.wait_send()
        send_gates(k, d).wait_send()
        return carry

    lax.fori_loop(0, 2 * STEPS, drain, 0)
    for store in stores:
        store.wait()


def body(rising, falling, rising_ids, falling_ids, norm_gain, router, w_gate, w_up, w_down):
    K = 2 * STEPS
    dma = pltpu.SemaphoreType.DMA
    any_space, vmem = pl.BlockSpec(memory_space=pl.ANY), pl.BlockSpec(memory_space=pltpu.VMEM)
    buffers = [
        ((K + 2, ROWS, QW), BF16),
        ((K, TOKS, TOP), jnp.int32),
        ((2, ROWS, QW), BF16),
        ((K, 4, UNIT, QW), BF16),
        ((K, 2, UNIT, QW), BF16),
        ((K, N_Y, 2, UNIT, QW), BF16),
        ((K, N_Y, 2, UNIT, QW), BF16),
        ((K, N_Y, 2, UNIT, QW), BF16),
        ((K, 2, 2, UNIT, QW), BF16),
        ((K + 2, 4, UNIT, QW), BF16),
        ((K, TOKS, 128), BF16),
        ((K + 2, TOKS, 128), BF16),
        ((PART, QW), BF16),
        ((PART, QW), BF16),
        ((ROWS, QW), F32),
        ((D, 4 * HID), BF16),
        ((2 * HID, D), BF16),
        ((PART, PART), BF16),
        ((PART, PART), BF16),
        ((2, N_Y, 2, 16, HALF), BF16),
        ((N_Q, EXPERTS, QW), BF16),
    ]
    semaphores = [
        (2, N_Q), (3,), (3,), (3,), (16,), (16,),
        (K, 2, 7), (K, 2, 7), (K, 2, 7), (K, 2, 7),
        (K,), (K,), (K,), (K,), (K, 2), (K, 2), (K,), (K,),
    ]
    return pl.pallas_call(
        kernel,
        out_shape=[jax.ShapeDtypeStruct(rising.shape, BF16)] * 2,
        in_specs=[any_space, any_space, vmem, vmem, vmem, vmem, any_space, any_space, any_space],
        out_specs=[any_space, any_space],
        scratch_shapes=[pltpu.VMEM(shape, dtype) for shape, dtype in buffers] + [dma(shape) for shape in semaphores],
        compiler_params=pltpu.CompilerParams(
            collective_id=0, has_side_effects=True, vmem_limit_bytes=56 * 1024 * 1024
        ),
        name="moe_relay",
    )(rising, falling, jnp.swapaxes(rising_ids, 2, 3), jnp.swapaxes(falling_ids, 2, 3), norm_gain, router, w_gate, w_up, w_down)


def solution(mesh):
    return jax.shard_map(
        body,
        mesh=mesh,
        in_specs=(
            P("pp", "ep", None),
            P("pp", "ep", None),
            P(None, "pp", "ep", None),
            P(None, "pp", "ep", None),
            P("pp", None),
            P("pp", "ep", None),
            P("pp", None, "ep"),
            P("pp", None, "ep"),
            P("pp", "ep", None),
        ),
        out_specs=(P("pp", "ep", None), P("pp", "ep", None)),
        check_vma=False,
    )
```
